256 devices in a mesh: tm: 4 (over z_hi), height: 16 (over y, z_lo, core), tensor: 4 (over x).
Axes of the slice: x: 4, y: 4, z: 8 (z_hi: 4, z_lo: 2; z = z_hi * 2 + z_lo), core: 2. Of those that a mesh axis runs over, the one named last changes fastest.
Arguments:
- tokens: bfloat16 [8, 64, 64, 1024], P('tm', 'height', None, 'tensor'), may hold values from -40 to 40
- cotangent: bfloat16 [8, 64, 64, 1024], P('tm', 'height', None, 'tensor'), may hold values from -6 to 6
- w_qkv: bfloat16 [1024, 3, 1024], P(None, None, 'tensor'), may hold values from -0.125 to 0.125
- w_out: bfloat16 [1024, 1024], P('tensor'), may hold values from -0.1875 to 0.1875
Outputs:
- mixed: bfloat16 [8, 64, 64, 1024], P('tm', 'height', None, 'tensor')
- in_grad: bfloat16 [8, 64, 64, 1024], P('tm', 'height', None, 'tensor')
The draws below stay inside these ranges and needn't reach their ends.
All inputs are finite; a program needn't handle non-finite values.
Results may differ from the reference program's by a relative error of at most 0.011.
Values may be sent and summed in bfloat16 or wider, within the bound.
No kernel may reach another device: no remote copies, remote signals or barrier semaphores. Data moves between devices by JAX's collectives and lax.ppermute only.
A program may use at most 128 MiB of HBM per device.

```python
import math
import jax
import jax.numpy as jnp
import numpy as np
from jax import lax

D = 1024
HEADS = 16
HEAD_SIZE = 64
COLS = 64
FRAMES = 8
ROWS = 64


def draw_tokens(key, part):
    key = jax.random.fold_in(key, 11)
    base_key = jax.random.fold_in(key, 0)
    base = jax.random.normal(base_key, (FRAMES, ROWS, COLS, D), jnp.float32)
    base = jnp.clip(base, -8.0, 8.0)
    return base.astype(jnp.bfloat16)


def draw_w_qkv(key, part):
    key = jax.random.fold_in(key, 23)
    bound = 4.0 * D ** (-0.5)
    raw = jax.random.normal(key, (D, 3, D), jnp.float32) * D ** (-0.5)
    raw = jnp.clip(raw, -bound, bound)
    return raw.astype(jnp.bfloat16)


def steps_of(key, dims, cuts, smallest, largest):
    def one(dim, shards_of):
        heights = jax.random.uniform(jax.random.fold_in(jax.random.fold_in(key, 6), dim), (shards_of,), jnp.float32, smallest / len(cuts), largest / len(cuts))
        return jnp.repeat(jnp.exp(heights), dims[dim] // shards_of).reshape((-1,) + (1,) * (len(dims) - dim - 1))

    loudness = one(*cuts[0])
    for cut in cuts[1:]:
        loudness = loudness * one(*cut)
    return loudness


def noise(key, dims, scale, reach, shards=(), kind=jnp.bfloat16):
    gain = steps_of(key, dims, shards, -0.22, 0.18) if shards else 1.0
    entries = jax.random.normal(key, dims, jnp.float32) * scale * gain
    return jnp.minimum(jnp.maximum(entries, -reach), reach).astype(kind)


def setup_inputs(seed: int = 0) -> dict:
    key_of = jax.random.split(jax.random.key(seed), 5)
    return {
        "tokens": draw_tokens(jax.random.fold_in(key_of[4], 71), 0),
        "cotangent": noise(key_of[1], (FRAMES, ROWS, COLS, D), 1.0, 6.0, ((0, 4), (1, 16), (3, 4))),
        "w_qkv": draw_w_qkv(jax.random.fold_in(key_of[4], 71), 0),
        "w_out": noise(key_of[3], (D, D), D ** -0.5, 0.1875, ((0, 4),)),
    }


NEG_FILL = -1e+30

def narrow(value):
    return lax.optimization_barrier(value.astype(jnp.bfloat16)).astype(jnp.float32)

def window_offsets():
    table = [(a, b, c) for a in range(3) for b in range(7) for c in range(7)]
    return jnp.asarray(np.array(table, dtype=np.int32))

def reference(tokens, cotangent, w_qkv, w_out):
    frames_all, rows_all, columns, width = tokens.shape
    count = frames_all * rows_all * columns
    grid = (frames_all, rows_all, columns, HEADS, HEAD_SIZE)
    scale = 1.0 / math.sqrt(HEAD_SIZE)
    flat_in = w_qkv.reshape(width, 3 * width)
    proj = narrow(jnp.dot(tokens.reshape(count, width), flat_in, preferred_element_type=jnp.float32))
    query = proj[:, :width].reshape(grid)
    keys = proj[:, width:2 * width].reshape(grid)
    values = proj[:, 2 * width:].reshape(grid)
    back = narrow(jnp.dot(cotangent.reshape(count, width), w_out.T, preferred_element_type=jnp.float32)).reshape(grid)
    spread = ((1, 1), (3, 3), (3, 3), (0, 0), (0, 0))
    key_pad = jnp.pad(keys, spread)
    value_pad = jnp.pad(values, spread)
    inside = jnp.pad(jnp.ones((frames_all, rows_all, columns), jnp.float32), spread[:3])
    offsets = window_offsets()
    anchor = jnp.int32(0)

    def moved(padded, offset):
        return lax.dynamic_slice(padded, (offset[0], offset[1], offset[2], anchor, anchor), grid)

    def score_at(offset):
        present = lax.dynamic_slice(inside, (offset[0], offset[1], offset[2]), grid[:3])[..., None] > 0.5
        raw = lax.optimization_barrier(jnp.sum(query * moved(key_pad, offset), axis=-1)) * scale
        return jnp.where(present, raw, NEG_FILL)
    scores = lax.map(score_at, offsets)
    top = lax.optimization_barrier(jnp.max(scores, axis=0))
    expo = jnp.exp(scores - top)
    probs = expo / lax.optimization_barrier(jnp.sum(expo, axis=0))
    probs_low = narrow(probs)

    def add_values(total, item):
        offset, weight = item
        return (total + weight[..., None] * moved(value_pad, offset), None)
    attended, _ = lax.scan(add_values, jnp.zeros(grid, jnp.float32), (offsets, probs_low))
    attended = attended.astype(jnp.bfloat16).reshape(count, width)
    mixed = jnp.dot(attended, w_out, preferred_element_type=jnp.float32).astype(jnp.bfloat16)

    def slope_at(offset):
        return lax.optimization_barrier(jnp.sum(back * moved(value_pad, offset), axis=-1))
    slopes = lax.map(slope_at, offsets)
    centre = lax.optimization_barrier(jnp.sum(probs * slopes, axis=0))
    dscore = narrow(probs * (slopes - centre) * scale)

    def add_keys(total, item):
        offset, weight = item
        return (total + weight[..., None] * moved(key_pad, offset), None)
    query_grad, _ = lax.scan(add_keys, jnp.zeros(grid, jnp.float32), (offsets, dscore))

    def scatter_back(carry, item):
        key_grad, value_grad = carry
        offset, weight, weight_low = item
        start = (offset[0], offset[1], offset[2], anchor, anchor)
        key_grad = lax.dynamic_update_slice(key_grad, lax.dynamic_slice(key_grad, start, grid) + weight[..., None] * query, start)
        value_grad = lax.dynamic_update_slice(value_grad, lax.dynamic_slice(value_grad, start, grid) + weight_low[..., None] * back, start)
        return ((key_grad, value_grad), None)
    blank = jnp.zeros(key_pad.shape, jnp.float32)
    (key_grad, value_grad), _ = lax.scan(scatter_back, (blank, blank), (offsets, dscore, probs_low))
    key_grad = key_grad[1:-1, 3:-3, 3:-3]
    value_grad = value_grad[1:-1, 3:-3, 3:-3]
    grads = jnp.concatenate([query_grad.astype(jnp.bfloat16).reshape(count, width), key_grad.astype(jnp.bfloat16).reshape(count, width), value_grad.astype(jnp.bfloat16).reshape(count, width)], axis=1)
    in_grad = jnp.dot(grads, flat_in.T, preferred_element_type=jnp.float32).astype(jnp.bfloat16)
    return (mixed.reshape(tokens.shape), in_grad.reshape(tokens.shape))
```

```python
import math

import jax
import jax.numpy as jnp
from jax import lax
from jax.experimental import pallas as pl
from jax.experimental.pallas import tpu as pltpu
from jax.sharding import PartitionSpec as P

NT = (((1,), (1,)), ((), ()))
NN = (((1,), (0,)), ((), ()))
F32, BF16 = jnp.float32, jnp.bfloat16
NEG_FILL = -1e30


def dot(a, b, dims=NN):
    return lax.dot_general(a, b, dims, preferred_element_type=F32)


def attend_body(valid, q, b, own, tmb, tma, hb, ha, bb, ba, ab, aa,
                att, dq, g_own, g_tmb, g_tma, g_hb, g_ha, g_bb, g_ba, g_ab, g_aa,
                ks, vs, kt, vt, dk, dv, s_buf, t_buf, p_buf, d_buf, bias):
    def put(frame, row, block):
        rows = block.shape[0]
        block = block.reshape(rows * 64, 512)
        at = pl.ds((frame * 10 + row) * 64, rows * 64)
        ks[at, :] = block[:, :256]
        vs[at, :] = block[:, 256:]

    for i in range(2):
        put(1 + i, 0, hb[i])
        put(1 + i, 3, own[i])
        put(1 + i, 7, ha[i])
    put(0, 0, bb[0])
    put(0, 3, tmb[0])
    put(0, 7, ba[0])
    put(3, 0, ab[0])
    put(3, 3, tma[0])
    put(3, 7, aa[0])

    row256 = lax.broadcasted_iota(jnp.int32, (256, 256), 0)
    lane256 = lax.broadcasted_iota(jnp.int32, (256, 256), 1)
    eye = jnp.where(row256 == lane256, 1.0, 0.0).astype(BF16)
    same_head = (row256 // 64) == (lane256 // 64)
    for i in range(5):
        at = pl.ds(i * 512, 512)
        kt[0, :, at] = dot(eye, ks[at, :], NT).astype(BF16)
        vt[0, :, at] = dot(eye, vs[at, :], NT).astype(BF16)
        width = 512 if i < 4 else 448
        src, dst = pl.ds(i * 512 + 64, width), pl.ds(i * 512, width)
        kt[1, :, dst] = dot(eye, ks[src, :], NT).astype(BF16)
        vt[1, :, dst] = dot(eye, vs[src, :], NT).astype(BF16)
    dk[...] = jnp.zeros_like(dk)
    dv[...] = jnp.zeros_like(dv)
    krow = lax.broadcasted_iota(jnp.int32, (64, 256), 0)
    qcol = lax.broadcasted_iota(jnp.int32, (64, 256), 1) % 64
    bias[0] = jnp.full((64, 256), NEG_FILL, F32)
    bias[1] = jnp.where(jnp.abs(krow - qcol) <= 3, 0.0, NEG_FILL)
    lane_head = lax.broadcasted_iota(jnp.int32, (64, 256), 1) // 64

    def spread(rows):
        return jnp.where(same_head, jnp.concatenate([rows] * 4, axis=0), jnp.zeros((), BF16))

    def gather(outT):
        out = outT.T
        res = out[0:64]
        for h in range(1, 4):
            res = jnp.where(lane_head == h, out[h * 64:(h + 1) * 64], res)
        return res

    def group(g, _):
        f, r = g // 4, g % 4
        par = r % 2
        mine = pl.ds(pl.multiple_of(g * 64, 64), 64)
        qbd = spread(q[mine, :])
        bbd = spread(b[mine, :])

        def rows_of(i):
            return pl.ds(pl.multiple_of(((f + i) * 10 + r) * 64, 64), 448)

        def lanes_of(i):
            return pl.ds(pl.multiple_of(((f + i) * 10 + r - par) * 64, 128), 448)

        top = jnp.full((64, 256), NEG_FILL, F32)
        for i in range(3):
            sc = dot(ks[rows_of(i), :], qbd, NT)
            for j in range(7):
                v = sc[j * 64:(j + 1) * 64] + bias[valid[f + i, r + j]]
                s_buf[pl.ds((i * 7 + j) * 64, 64), :] = v
                top = jnp.maximum(top, v)
        m = jnp.max(top, axis=0, keepdims=True)
        tot = jnp.zeros((64, 256), F32)
        for j in range(21):
            at = pl.ds(j * 64, 64)
            e = jnp.exp(s_buf[at, :] - m)
            s_buf[at, :] = e
            tot = tot + e
        inv = 1.0 / jnp.sum(tot, axis=0, keepdims=True)
        cen = jnp.zeros((64, 256), F32)
        for i in range(3):
            sl = dot(vs[rows_of(i), :], bbd, NT)
            for j in range(7):
                at = pl.ds((i * 7 + j) * 64, 64)
                p = s_buf[at, :] * inv
                s_buf[at, :] = p
                p_buf[at, :] = p.astype(BF16)
                x = sl[j * 64:(j + 1) * 64]
                t_buf[at, :] = x
                cen = cen + p * x
        c = jnp.sum(cen, axis=0, keepdims=True)
        for j in range(21):
            at = pl.ds(j * 64, 64)
            d_buf[at, :] = (s_buf[at, :] * (t_buf[at, :] - c)).astype(BF16)
        outT = jnp.zeros((256, 256), F32)
        dqT = jnp.zeros((256, 256), F32)
        for i in range(3):
            at = pl.ds(i * 448, 448)
            pb, db = p_buf[at, :], d_buf[at, :]
            outT = outT + dot(vt[par, :, lanes_of(i)], pb)
            dqT = dqT + dot(kt[par, :, lanes_of(i)], db)
            dv[rows_of(i), :] += dot(pb, bbd)
            dk[rows_of(i), :] += dot(db, qbd)
        att[mine, :] = gather(outT).astype(BF16)
        dq[mine, :] = (gather(dqT) * 0.125).astype(BF16)
        return 0

    lax.fori_loop(0, 8, group, 0)

    def take(frame, row, rows, out):
        at = pl.ds((frame * 10 + row) * 64, rows * 64)
        kv = jnp.concatenate([dk[at, :], dv[at, :]], axis=1)
        return kv.reshape(rows, 64, 512).astype(out.dtype)

    for i in range(2):
        g_hb[i] = take(1 + i, 0, 3, g_hb)
        g_own[i] = take(1 + i, 3, 4, g_own)
        g_ha[i] = take(1 + i, 7, 3, g_ha)
    g_bb[0] = take(0, 0, 3, g_bb)
    g_tmb[0] = take(0, 3, 4, g_tmb)
    g_ba[0] = take(0, 7, 3, g_ba)
    g_ab[0] = take(3, 0, 3, g_ab)
    g_tma[0] = take(3, 3, 4, g_tma)
    g_aa[0] = take(3, 7, 3, g_aa)


def attend(valid, q, b, own, pieces):
    S = jax.ShapeDtypeStruct
    frame, rows, corner = (1, 4, 64, 512), (2, 3, 64, 512), (1, 3, 64, 512)
    outs = (S((512, 256), BF16), S((512, 256), BF16), S((2, 4, 64, 512), F32),
            S(frame, BF16), S(frame, BF16), S(rows, BF16), S(rows, BF16),
            S(corner, BF16), S(corner, BF16), S(corner, BF16), S(corner, BF16))
    vm = pl.BlockSpec(memory_space=pltpu.VMEM)
    return pl.pallas_call(
        attend_body,
        out_shape=outs,
        in_specs=[pl.BlockSpec(memory_space=pltpu.SMEM)] + [vm] * 11,
        out_specs=(vm,) * 11,
        scratch_shapes=[
            pltpu.VMEM((2560, 256), BF16), pltpu.VMEM((2560, 256), BF16),
            pltpu.VMEM((2, 256, 2560), BF16), pltpu.VMEM((2, 256, 2560), BF16),
            pltpu.VMEM((2560, 256), F32), pltpu.VMEM((2560, 256), F32),
            pltpu.VMEM((1344, 256), F32), pltpu.VMEM((1344, 256), F32),
            pltpu.VMEM((1344, 256), BF16), pltpu.VMEM((1344, 256), BF16),
            pltpu.VMEM((2, 64, 256), F32),
        ],
        compiler_params=pltpu.CompilerParams(vmem_limit_bytes=32 * 1024 * 1024),
        cost_estimate=pl.CostEstimate(
            flops=8 * 6 * 2 * 1344 * 256 * 256, bytes_accessed=12 * 2**20, transcendentals=8 * 1344 * 256
        ),
        name="attend",
    )(valid, q, b, own, *pieces)


def project_body(idx, x0, x1, x2, x3, w, q, own, f0, f1, lo, hi, c0lo, c0hi, c1lo, c1hi):
    acc = None
    for i, x in enumerate((x0, x1, x2, x3)):
        at = pl.ds(pl.multiple_of(idx[i] * 256, 256), 256)
        part = [dot(x[...], w[n, at, :]) for n in range(3)]
        acc = part if acc is None else [a + b for a, b in zip(acc, part)]
    q[...] = acc[0].astype(BF16) * jnp.asarray(0.125, BF16)
    kv = jnp.concatenate([acc[1], acc[2]], axis=1).astype(BF16).reshape(2, 4, 64, 512)
    own[...] = kv
    f0[...] = kv[0:1]
    f1[...] = kv[1:2]
    lo[...] = kv[:, 0:3]
    hi[...] = kv[:, 1:4]
    c0lo[...] = kv[0:1, 0:3]
    c0hi[...] = kv[0:1, 1:4]
    c1lo[...] = kv[1:2, 0:3]
    c1hi[...] = kv[1:2, 1:4]


def back_body(idx, x0, x1, x2, x3, w, out):
    acc = None
    for i, x in enumerate((x0, x1, x2, x3)):
        part = dot(x[...], w[:, pl.ds(pl.multiple_of(idx[i] * 256, 256), 256)], NT)
        acc = part if acc is None else acc + part
    out[...] = acc.astype(BF16)


def mixed_body(idx, att, w, own, right, left, across):
    for i, out in enumerate((own, right, left, across)):
        block = w[:, pl.ds(pl.multiple_of(idx[i] * 256, 256), 256)]
        out[...] = dot(att[...], block).astype(out.dtype)


def grad_body(idx, dq, own, r1, r2, r3, r4, r5, r6, r7, r8, w, mine, right, left, across, kv):
    kv[...] = own[...]
    kv[1] += r1[0].astype(F32)
    kv[0] += r2[0].astype(F32)
    kv[:, 1:4] += r3[...].astype(F32)
    kv[:, 0:3] += r4[...].astype(F32)
    kv[1, 1:4] += r5[0].astype(F32)
    kv[1, 0:3] += r6[0].astype(F32)
    kv[0, 1:4] += r7[0].astype(F32)
    kv[0, 0:3] += r8[0].astype(F32)
    low = kv[...].reshape(512, 512).astype(BF16)
    for i, out in enumerate((mine, right, left, across)):
        at = pl.ds(pl.multiple_of(idx[i] * 256, 256), 256)
        total = dot(dq[...], w[0, at, :], NT)
        total = total + dot(low[:, :256], w[1, at, :], NT)
        total = total + dot(low[:, 256:], w[2, at, :], NT)
        out[...] = total.astype(out.dtype)


def sum_body(a, b, c, d, out):
    total = a[...] + b[...].astype(F32) + c[...].astype(F32) + d[...].astype(F32)
    out[...] = total.astype(BF16).reshape(out.shape)


def local_call(body, outs, idx, arrays, scratch=(), flops=0, name=None):
    vm = pl.BlockSpec(memory_space=pltpu.VMEM)
    specs = [vm] * len(arrays)
    args = list(arrays)
    if idx is not None:
        specs = [pl.BlockSpec(memory_space=pltpu.SMEM)] + specs
        args = [idx] + args
    size = sum(math.prod(a.shape) * a.dtype.itemsize for a in list(arrays) + list(outs))
    return pl.pallas_call(
        body,
        out_shape=tuple(outs),
        in_specs=specs,
        out_specs=(vm,) * len(outs),
        scratch_shapes=list(scratch),
        compiler_params=pltpu.CompilerParams(vmem_limit_bytes=24 * 1024 * 1024),
        cost_estimate=pl.CostEstimate(flops=flops, bytes_accessed=size, transcendentals=0),
        name=name,
    )(*args)


def shards(tokens, cotangent, w_qkv, w_out):
    S = jax.ShapeDtypeStruct
    n_x, n_t, n_h = (lax.axis_size(a) for a in ("tensor", "tm", "height"))
    x, t, h = (lax.axis_index(a) for a in ("tensor", "tm", "height"))
    idx = jnp.stack([x, (x + n_x - 1) % n_x, (x + 1) % n_x, (x + 2) % n_x]).astype(jnp.int32)
    idx_out = jnp.stack([x, (x + 1) % n_x, (x + n_x - 1) % n_x, (x + 2) % n_x]).astype(jnp.int32)
    frame_place = t * 2 + jnp.arange(4, dtype=jnp.int32) - 1
    row_place = h * 4 + jnp.arange(10, dtype=jnp.int32) - 3
    fine = ((frame_place >= 0) & (frame_place < 2 * n_t))[:, None]
    fine = fine & ((row_place >= 0) & (row_place < 4 * n_h))[None, :]
    valid = fine.astype(jnp.int32)

    def ring(array, by):
        return lax.ppermute(array, "tensor", [(i, (i + by) % n_x) for i in range(n_x)])

    def shift(array, dt, dh):
        pairs = [
            (i * n_h + j, ((i + dt) % n_t) * n_h + (j + dh) % n_h)
            for i in range(n_t)
            for j in range(n_h)
        ]
        return lax.ppermute(array, ("tm", "height"), pairs)

    tok = tokens.reshape(512, 256)
    flat = jnp.transpose(w_qkv, (1, 0, 2))
    t_parts = (ring(tok, 1), ring(tok, -1), ring(tok, 2))
    frame, rows, corner = (1, 4, 64, 512), (2, 3, 64, 512), (1, 3, 64, 512)
    q, own, f0, f1, lo, hi, c0lo, c0hi, c1lo, c1hi = local_call(
        project_body,
        (S((512, 256), BF16), S((2, 4, 64, 512), BF16), S(frame, BF16), S(frame, BF16),
         S(rows, BF16), S(rows, BF16), S(corner, BF16), S(corner, BF16), S(corner, BF16),
         S(corner, BF16)),
        idx, (tok, *t_parts, flat), flops=2 * 512 * 1024 * 768, name="project",
    )
    cot, _ = lax.optimization_barrier((cotangent.reshape(512, 256), t_parts[2]))
    c_parts = (ring(cot, 1), ring(cot, -1), ring(cot, 2))
    pieces = (
        shift(f1, 1, 0), shift(f0, -1, 0), shift(hi, 0, 1), shift(lo, 0, -1),
        shift(c1hi, 1, 1), shift(c1lo, 1, -1), shift(c0hi, -1, 1), shift(c0lo, -1, -1),
    )
    (b,) = local_call(
        back_body, (S((512, 256), BF16),), idx, (cot, *c_parts, w_out),
        flops=2 * 512 * 1024 * 256, name="back",
    )
    att, dq, g_own, g_tmb, g_tma, g_hb, g_ha, g_bb, g_ba, g_ab, g_aa = attend(
        valid, q, b, own, pieces
    )
    returned = (
        shift(g_tmb, -1, 0), shift(g_tma, 1, 0), shift(g_hb, 0, -1), shift(g_ha, 0, 1),
        shift(g_bb, -1, -1), shift(g_ba, -1, 1), shift(g_ab, 1, -1), shift(g_aa, 1, 1),
    )
    piece = S((512, 256), BF16)
    parts = (S((512, 256), F32), piece, piece, piece)
    m0, m1, m2, m3 = local_call(
        mixed_body, parts, idx_out, (att, w_out), flops=2 * 512 * 1024 * 256, name="mix",
    )
    out = (S((2, 4, 64, 256), BF16),)
    (mixed,) = local_call(sum_body, out, None, (m0, ring(m1, 1), ring(m2, -1), ring(m3, 2)), name="mixed_sum")
    g0, g1, g2, g3 = local_call(
        grad_body, parts, idx_out, (dq, g_own, *returned, flat),
        scratch=[pltpu.VMEM((2, 4, 64, 512), F32)], flops=2 * 512 * 1024 * 768, name="in_grad",
    )
    (in_grad,) = local_call(sum_body, out, None, (g0, ring(g1, 1), ring(g2, -1), ring(g3, 2)), name="in_grad_sum")
    return mixed, in_grad


def solution(mesh):
    in_specs = (
        P("tm", "height", None, "tensor"),
        P("tm", "height", None, "tensor"),
        P(None, None, "tensor"),
        P("tensor", None),
    )
    out_specs = (P("tm", "height", None, "tensor"), P("tm", "height", None, "tensor"))
    return jax.shard_map(shards, mesh=mesh, in_specs=in_specs, out_specs=out_specs, check_vma=False)
```

```python
import math

import jax
import jax.numpy as jnp
from jax import lax
from jax.experimental import pallas as pl
from jax.experimental.pallas import tpu as pltpu
from jax.sharding import PartitionSpec as P

NT = (((1,), (1,)), ((), ()))
NN = (((1,), (0,)), ((), ()))
F32, BF16 = jnp.float32, jnp.bfloat16
NEG_FILL = -1e30
MIB = 1024 * 1024


def dot(a, b, dims=NN):
    return lax.dot_general(a, b, dims, preferred_element_type=F32)


def attend_body(valid, q, b, own, tmb, tma, hb, ha,
                att, dq, g_own, g_tmb, g_tma, g_hb, g_ha,
                ks, vs, kt, vt, dk, dv, s_buf, t_buf, p_buf, d_buf, bias):
    def put(frame, row, block):
        rows = block.shape[0]
        block = block.reshape(rows * 64, 256)
        at = pl.ds((frame * 10 + row) * 64, rows * 64)
        ks[at, :] = block[:, :128]
        vs[at, :] = block[:, 128:]

    for i in range(4):
        put(i, 0, hb[i])
        put(i, 7, ha[i])
    put(0, 3, tmb[0])
    put(1, 3, own[0])
    put(2, 3, own[1])
    put(3, 3, tma[0])

    eye = jnp.where(
        lax.broadcasted_iota(jnp.int32, (128, 128), 0) == lax.broadcasted_iota(jnp.int32, (128, 128), 1),
        1.0, 0.0,
    ).astype(BF16)
    same_head = (lax.broadcasted_iota(jnp.int32, (256, 128), 0) // 128) == (
        lax.broadcasted_iota(jnp.int32, (256, 128), 1) // 64
    )
    for i in range(5):
        at = pl.ds(i * 512, 512)
        kt[:, at] = dot(eye, ks[at, :], NT).astype(BF16)
        vt[:, at] = dot(eye, vs[at, :], NT).astype(BF16)
    dk[...] = jnp.zeros_like(dk)
    dv[...] = jnp.zeros_like(dv)
    krow = lax.broadcasted_iota(jnp.int32, (64, 256), 0)
    lane = lax.broadcasted_iota(jnp.int32, (64, 256), 1)
    band = jnp.abs(krow - lane % 64) <= 3
    second = (lane // 64) % 2 == 1
    bias[0] = jnp.full((64, 256), NEG_FILL, F32)
    bias[1] = jnp.where(band, 0.0, NEG_FILL)
    bias[2] = jnp.where(band & ~second, 0.0, NEG_FILL)
    bias[3] = jnp.where(band & second, 0.0, NEG_FILL)
    first_head = lax.broadcasted_iota(jnp.int32, (128, 128), 1) < 64

    def spread(rows):
        return jnp.where(same_head, jnp.concatenate([rows] * 2, axis=0), jnp.zeros((), BF16))

    def gather(outT):
        out = outT.T
        return jnp.where(first_head, out[0:128], out[128:256])

    def group(g, _):
        f, r = g // 2, (g % 2) * 2
        mine = pl.ds(pl.multiple_of(g * 128, 128), 128)
        qbd = spread(q[mine, :])
        bbd = spread(b[mine, :])

        def keys_of(i):
            return pl.ds(pl.multiple_of(((f + i) * 10 + r) * 64, 128), 512)

        top = jnp.full((64, 256), NEG_FILL, F32)
        for i in range(3):
            sc = dot(ks[keys_of(i), :], qbd, NT)
            for j in range(8):
                kind = 2 if j == 0 else 3 if j == 7 else 1
                v = sc[j * 64:(j + 1) * 64] + bias[valid[f + i, r + j] * kind]
                s_buf[pl.ds((i * 8 + j) * 64, 64), :] = v
                top = jnp.maximum(top, v)
        m = jnp.max(top, axis=0, keepdims=True)
        tot = jnp.zeros((64, 256), F32)
        for j in range(24):
            at = pl.ds(j * 64, 64)
            e = jnp.exp(s_buf[at, :] - m)
            s_buf[at, :] = e
            tot = tot + e
        inv = 1.0 / jnp.sum(tot, axis=0, keepdims=True)
        cen = jnp.zeros((64, 256), F32)
        for i in range(3):
            sl = dot(vs[keys_of(i), :], bbd, NT)
            for j in range(8):
                at = pl.ds((i * 8 + j) * 64, 64)
                p = s_buf[at, :] * inv
                s_buf[at, :] = p
                p_buf[at, :] = p.astype(BF16)
                x = sl[j * 64:(j + 1) * 64]
                t_buf[at, :] = x
                cen = cen + p * x
        c = jnp.sum(cen, axis=0, keepdims=True)
        for j in range(24):
            at = pl.ds(j * 64, 64)
            d_buf[at, :] = (s_buf[at, :] * (t_buf[at, :] - c)).astype(BF16)
        outT = jnp.zeros((128, 256), F32)
        dqT = jnp.zeros((128, 256), F32)
        for i in range(3):
            at = pl.ds(i * 512, 512)
            pb, db = p_buf[at, :], d_buf[at, :]
            outT = outT + dot(vt[:, keys_of(i)], pb)
            dqT = dqT + dot(kt[:, keys_of(i)], db)
            dv[keys_of(i), :] += dot(pb, bbd)
            dk[keys_of(i), :] += dot(db, qbd)
        att[mine, :] = gather(outT).astype(BF16)
        dq[mine, :] = (gather(dqT) * 0.125).astype(BF16)
        return 0

    lax.fori_loop(0, 4, group, 0)

    def take(frame, row, rows, out):
        at = pl.ds((frame * 10 + row) * 64, rows * 64)
        kv = jnp.concatenate([dk[at, :], dv[at, :]], axis=1)
        return kv.reshape(rows, 64, 256).astype(out.dtype)

    for i in range(4):
        g_hb[i] = take(i, 0, 3, g_hb)
        g_ha[i] = take(i, 7, 3, g_ha)
    g_tmb[0] = take(0, 3, 4, g_tmb)
    g_own[0] = take(1, 3, 4, g_own)
    g_own[1] = take(2, 3, 4, g_own)
    g_tma[0] = take(3, 3, 4, g_tma)


def project_body(idx, x0, x1, x2, x3, w, q0, q1, own0, own1, f00, f10, f01, f11):
    acc = None
    for i, x in enumerate((x0, x1, x2, x3)):
        at = pl.ds(pl.multiple_of(idx[i] * 256, 256), 256)
        part = [dot(x[...], w[n, at, :]) for n in range(3)]
        acc = part if acc is None else [a + b for a, b in zip(acc, part)]
    query, keys, values = (a.astype(BF16) for a in acc)
    query = query * jnp.asarray(0.125, BF16)
    for half, (q, own, f0, f1) in enumerate(((q0, own0, f00, f10), (q1, own1, f01, f11))):
        at = slice(half * 128, half * 128 + 128)
        q[...] = query[:, at]
        kv = jnp.concatenate([keys[:, at], values[:, at]], axis=1).reshape(2, 4, 64, 256)
        own[...] = kv
        f0[...] = kv[0:1]
        f1[...] = kv[1:2]


def edges_body(tmb, own, tma, lo, hi):
    for i, (ref, at) in enumerate(((tmb, 0), (own, 0), (own, 1), (tma, 0))):
        lo[i] = ref[at, 0:3]
        hi[i] = ref[at, 1:4]


def fold_body(g_tmb, g_tma, r_hb, r_ha, s_tmb, s_tma, acc):
    for g, at, s in ((g_tmb, 0, s_tmb), (g_tma, 3, s_tma)):
        acc[...] = g[...]
        acc[0, 0:3] += r_hb[at].astype(F32)
        acc[0, 1:4] += r_ha[at].astype(F32)
        s[...] = acc[...].astype(BF16)


def back_body(idx, x0, x1, x2, x3, w, out0, out1):
    acc = None
    for i, x in enumerate((x0, x1, x2, x3)):
        part = dot(x[...], w[:, pl.ds(pl.multiple_of(idx[i] * 256, 256), 256)], NT)
        acc = part if acc is None else acc + part
    out0[...] = acc[:, :128].astype(BF16)
    out1[...] = acc[:, 128:].astype(BF16)


def mixed_body(idx, att0, att1, w, own, right, left, across):
    att = jnp.concatenate([att0[...], att1[...]], axis=1)
    for i, out in enumerate((own, right, left, across)):
        block = w[:, pl.ds(pl.multiple_of(idx[i] * 256, 256), 256)]
        out[...] = dot(att, block).astype(out.dtype)


def grad_body(idx, dq0, own0, hb0, ha0, tb0, ta0, dq1, own1, hb1, ha1, tb1, ta1, w,
              mine, right, left, across, kv):
    low = []
    for own, hb, ha, tb, ta in ((own0, hb0, ha0, tb0, ta0), (own1, hb1, ha1, tb1, ta1)):
        kv[...] = own[...]
        kv[:, 0:3] += hb[1:3].astype(F32)
        kv[:, 1:4] += ha[1:3].astype(F32)
        kv[0] += tb[0].astype(F32)
        kv[1] += ta[0].astype(F32)
        low.append(kv[...].reshape(512, 256).astype(BF16))
    dq = jnp.concatenate([dq0[...], dq1[...]], axis=1)
    dk = jnp.concatenate([low[0][:, :128], low[1][:, :128]], axis=1)
    dv = jnp.concatenate([low[0][:, 128:], low[1][:, 128:]], axis=1)
    for i, out in enumerate((mine, right, left, across)):
        at = pl.ds(pl.multiple_of(idx[i] * 256, 256), 256)
        total = dot(dq, w[0, at, :], NT)
        total = total + dot(dk, w[1, at, :], NT)
        total = total + dot(dv, w[2, at, :], NT)
        out[...] = total.astype(out.dtype)


def sum_body(a, b, c, d, out):
    total = a[...] + b[...].astype(F32) + c[...].astype(F32) + d[...].astype(F32)
    out[...] = total.astype(BF16).reshape(out.shape)


def local_call(body, outs, idx, arrays, scratch=(), flops=0, name=None, limit=12):
    vm = pl.BlockSpec(memory_space=pltpu.VMEM)
    specs = [vm] * len(arrays)
    args = list(arrays)
    if idx is not None:
        specs = [pl.BlockSpec(memory_space=pltpu.SMEM)] + specs
        args = [idx] + args
    size = sum(math.prod(a.shape) * a.dtype.itemsize for a in list(arrays) + list(outs))
    return pl.pallas_call(
        body,
        out_shape=tuple(outs),
        in_specs=specs,
        out_specs=(vm,) * len(outs),
        scratch_shapes=list(scratch),
        compiler_params=pltpu.CompilerParams(vmem_limit_bytes=limit * MIB),
        cost_estimate=pl.CostEstimate(flops=flops, bytes_accessed=size, transcendentals=0),
        name=name,
    )(*args)


def shards(tokens, cotangent, w_qkv, w_out):
    S = jax.ShapeDtypeStruct
    n_x, n_t, n_h = (lax.axis_size(a) for a in ("tensor", "tm", "height"))
    x, t, h = (lax.axis_index(a) for a in ("tensor", "tm", "height"))
    idx = jnp.stack([x, (x + n_x - 1) % n_x, (x + 1) % n_x, (x + 2) % n_x]).astype(jnp.int32)
    idx_out = jnp.stack([x, (x + 1) % n_x, (x + n_x - 1) % n_x, (x + 2) % n_x]).astype(jnp.int32)
    frame_place = t * 2 + jnp.arange(4, dtype=jnp.int32) - 1
    row_place = h * 4 + jnp.arange(10, dtype=jnp.int32) - 3
    fine = ((frame_place >= 0) & (frame_place < 2 * n_t))[:, None]
    fine = fine & ((row_place >= 0) & (row_place < 4 * n_h))[None, :]
    valid = fine.astype(jnp.int32)

    def ring(array, by):
        return lax.ppermute(array, "tensor", [(i, (i + by) % n_x) for i in range(n_x)])

    def frames(array, by):
        return lax.ppermute(array, "tm", [(i, (i + by) % n_t) for i in range(n_t)])

    def rows(array, by):
        return lax.ppermute(array, "height", [(i, (i + by) % n_h) for i in range(n_h)])

    tok = tokens.reshape(512, 256)
    flat = jnp.transpose(w_qkv, (1, 0, 2))
    t_parts = (ring(tok, 1), ring(tok, -1), ring(tok, 2))
    half = S((512, 128), BF16)
    pair, frame, edge = (2, 4, 64, 256), (1, 4, 64, 256), (4, 3, 64, 256)
    q0, q1, own0, own1, f00, f10, f01, f11 = local_call(
        project_body,
        (half, half, S(pair, BF16), S(pair, BF16)) + (S(frame, BF16),) * 4,
        idx, (tok, *t_parts, flat), flops=2 * 512 * 1024 * 768, name="project",
    )
    cot, _ = lax.optimization_barrier((cotangent.reshape(512, 256), q0))

    def surround(own, f0, f1):
        tmb, tma = frames(f1, 1), frames(f0, -1)
        lo, hi = local_call(edges_body, (S(edge, BF16),) * 2, None, (tmb, own, tma), name="edges")
        return own, tmb, tma, rows(hi, 1), rows(lo, -1)

    around0 = surround(own0, f00, f10)
    c_parts = (ring(cot, 1), ring(cot, -1), ring(cot, 2))
    around1 = surround(own1, f01, f11)
    b0, b1 = local_call(
        back_body, (half, half), idx, (cot, *c_parts, w_out),
        flops=2 * 512 * 1024 * 256, name="back",
    )

    def attend(q, b, around):
        return local_call(
            attend_body,
            (half, half, S(pair, F32), S(frame, F32), S(frame, F32), S(edge, BF16), S(edge, BF16)),
            valid, (q, b, *around),
            scratch=[
                pltpu.VMEM((2560, 128), BF16), pltpu.VMEM((2560, 128), BF16),
                pltpu.VMEM((128, 2560), BF16), pltpu.VMEM((128, 2560), BF16),
                pltpu.VMEM((2560, 128), F32), pltpu.VMEM((2560, 128), F32),
                pltpu.VMEM((1536, 256), F32), pltpu.VMEM((1536, 256), F32),
                pltpu.VMEM((1536, 256), BF16), pltpu.VMEM((1536, 256), BF16),
                pltpu.VMEM((4, 64, 256), F32),
            ],
            flops=4 * 6 * 2 * 1536 * 256 * 256 * 2, name="attend", limit=24,
        )

    def settle(g_tmb, g_tma, g_hb, g_ha):
        r_ha, r_hb = rows(g_hb, -1), rows(g_ha, 1)
        s_tmb, s_tma = local_call(
            fold_body, (S(frame, BF16),) * 2, None, (g_tmb, g_tma, r_hb, r_ha),
            scratch=[pltpu.VMEM(frame, F32)], name="fold",
        )
        return r_hb, r_ha, frames(s_tma, 1), frames(s_tmb, -1)

    att0, dq0, g_own0, *g0 = attend(q0, b0, around0)
    att1, dq1, g_own1, *g1 = attend(q1, b1, around1)
    back0 = settle(*g0)
    back1 = settle(*g1)
    piece = S((512, 256), BF16)
    parts = (S((512, 256), F32), piece, piece, piece)
    m0, m1, m2, m3 = local_call(
        mixed_body, parts, idx_out, (att0, att1, w_out), flops=2 * 512 * 1024 * 256, name="mix",
    )
    out = (S((2, 4, 64, 256), BF16),)
    (mixed,) = local_call(
        sum_body, out, None, (m0, ring(m1, 1), ring(m2, -1), ring(m3, 2)), name="mixed_sum"
    )
    e0, e1, e2, e3 = local_call(
        grad_body, parts, idx_out, (dq0, g_own0, *back0, dq1, g_own1, *back1, flat),
        scratch=[pltpu.VMEM(pair, F32)], flops=2 * 512 * 1024 * 768, name="in_grad", limit=16,
    )
    (in_grad,) = local_call(
        sum_body, out, None, (e0, ring(e1, 1), ring(e2, -1), ring(e3, 2)), name="in_grad_sum"
    )
    return mixed, in_grad


def solution(mesh):
    in_specs = (
        P("tm", "height", None, "tensor"),
        P("tm", "height", None, "tensor"),
        P(None, None, "tensor"),
        P("tensor", None),
    )
    out_specs = (P("tm", "height", None, "tensor"), P("tm", "height", None, "tensor"))
    return jax.shard_map(shards, mesh=mesh, in_specs=in_specs, out_specs=out_specs, check_vma=False)
```

```python
import functools
import math

import jax
import jax.numpy as jnp
from jax import lax
from jax.experimental import pallas as pl
from jax.experimental.pallas import tpu as pltpu
from jax.sharding import PartitionSpec as P

NT = (((1,), (1,)), ((), ()))
NN = (((1,), (0,)), ((), ()))
F32, BF16 = jnp.float32, jnp.bfloat16
NEG_FILL = -1e30
MIB = 1024 * 1024


def dot(a, b, dims=NN):
    return lax.dot_general(a, b, dims, preferred_element_type=F32)


def attend_body(half, valid, q, b, f0, f1, tmb, tma, hb, ha,
                att, dq, g_own, g_tmb, g_tma, g_hb, g_ha,
                ks, vs, kt, vt, dk, dv, s_buf0, s_buf1, p_buf0, p_buf1, d_buf0, d_buf1, bias):
    def put(frame, row, block):
        rows = block.shape[0]
        block = block.reshape(rows * 64, 256)
        at = pl.ds((frame * 10 + row) * 64, rows * 64)
        ks[at, :] = block[:, :128]
        vs[at, :] = block[:, 128:]

    for i in range(4):
        put(i, 0, hb[i])
        put(i, 7, ha[i])
    lanes = pl.ds(half * 256, 256)
    for i, ref in enumerate((tmb, f0, f1, tma)):
        put(i, 3, ref[0, :, :, lanes])

    eye = jnp.where(
        lax.broadcasted_iota(jnp.int32, (128, 128), 0) == lax.broadcasted_iota(jnp.int32, (128, 128), 1),
        1.0, 0.0,
    ).astype(BF16)
    same_head = (lax.broadcasted_iota(jnp.int32, (256, 128), 0) // 128) == (
        lax.broadcasted_iota(jnp.int32, (256, 128), 1) // 64
    )
    for i in range(5):
        at = pl.ds(i * 512, 512)
        kt[:, at] = ks[at, :].T
        vt[:, at] = vs[at, :].T
    krow = lax.broadcasted_iota(jnp.int32, (64, 256), 0)
    lane = lax.broadcasted_iota(jnp.int32, (64, 256), 1)
    band = jnp.abs(krow - lane % 64) <= 3
    second = (lane // 64) % 2 == 1
    bias[0] = jnp.full((64, 256), NEG_FILL, F32)
    bias[1] = jnp.where(band, 0.0, NEG_FILL)
    bias[2] = jnp.where(band & ~second, 0.0, NEG_FILL)
    bias[3] = jnp.where(band & second, 0.0, NEG_FILL)
    first_head = lax.broadcasted_iota(jnp.int32, (128, 128), 1) < 64

    def spread(rows):
        return jnp.where(same_head, jnp.concatenate([rows] * 2, axis=0), jnp.zeros((), BF16))

    def gather(outT):
        out = outT.T
        return jnp.where(first_head, out[0:128], out[128:256])

    bufs = ((s_buf0, p_buf0, d_buf0), (s_buf1, p_buf1, d_buf1))

    def span(g, i):
        f, r = g // 2, (g % 2) * 2
        return ((f + i) * 10 + r) * 64

    def keys_of(g, i):
        return pl.ds(span(g, i), 512)

    def add_to(ref, g, i, term):
        f, r = g // 2, (g % 2) * 2
        seen = 6 if r == 2 else 0
        if f == 1 and i < 2:
            seen = 8
        at = span(g, i)
        if seen:
            ref[pl.ds(at, seen * 64), :] += term[: seen * 64]
        if seen < 8:
            ref[pl.ds(at + seen * 64, 512 - seen * 64), :] = term[seen * 64:]

    def scores(g):
        s_buf = bufs[g % 2][0]
        f, r = g // 2, (g % 2) * 2
        qbd = spread(q[pl.ds(g * 128, 128), :])
        top = jnp.full((64, 256), NEG_FILL, F32)
        for i in range(3):
            sc = dot(ks[keys_of(g, i), :], qbd, NT)
            for j in range(8):
                kind = 2 if j == 0 else 3 if j == 7 else 1
                v = sc[j * 64:(j + 1) * 64] + bias[valid[f + i, r + j] * kind]
                s_buf[pl.ds((i * 8 + j) * 64, 64), :] = v
                top = jnp.maximum(top, v)
        return jnp.max(top, axis=0, keepdims=True)

    def weights(g, m):
        s_buf, p_buf, _ = bufs[g % 2]
        tot = jnp.zeros((64, 256), F32)
        for j in range(24):
            at = pl.ds(j * 64, 64)
            e = jnp.exp(s_buf[at, :] - m)
            s_buf[at, :] = e
            tot = tot + e
        inv = 1.0 / jnp.sum(tot, axis=0, keepdims=True)
        for j in range(24):
            at = pl.ds(j * 64, 64)
            p_buf[at, :] = (s_buf[at, :] * inv).astype(BF16)
        return inv

    def values(g):
        p_buf = bufs[g % 2][1]
        mine = pl.ds(g * 128, 128)
        bbd = spread(b[mine, :])
        outT = jnp.zeros((128, 256), F32)
        for i in range(3):
            pb = p_buf[pl.ds(i * 512, 512), :]
            outT = outT + dot(vt[:, keys_of(g, i)], pb)
            add_to(dv, g, i, dot(pb, bbd))
        att[mine, :] = gather(outT).astype(BF16)
        return jnp.sum(outT * dot(eye, bbd, NT), axis=0, keepdims=True)

    def slopes(g, inv, c):
        s_buf, _, d_buf = bufs[g % 2]
        bbd = spread(b[pl.ds(g * 128, 128), :])
        for i in range(3):
            sl = dot(vs[keys_of(g, i), :], bbd, NT)
            for j in range(8):
                at = pl.ds((i * 8 + j) * 64, 64)
                d_buf[at, :] = (s_buf[at, :] * inv * (sl[j * 64:(j + 1) * 64] - c)).astype(BF16)

    def grads(g):
        d_buf = bufs[g % 2][2]
        mine = pl.ds(g * 128, 128)
        qbd = spread(q[mine, :])
        dqT = jnp.zeros((128, 256), F32)
        for i in range(3):
            db = d_buf[pl.ds(i * 512, 512), :]
            dqT = dqT + dot(kt[:, keys_of(g, i)], db)
            add_to(dk, g, i, dot(db, qbd))
        dq[mine, :] = (gather(dqT) * 0.125).astype(BF16)

    m = scores(0)
    for g in range(4):
        inv = weights(g, m)
        if g > 0:
            grads(g - 1)
        if g < 3:
            m = scores(g + 1)
        c = values(g)
        slopes(g, inv, c)
    grads(3)

    def take(frame, row, rows, out):
        at = pl.ds((frame * 10 + row) * 64, rows * 64)
        kv = jnp.concatenate([dk[at, :], dv[at, :]], axis=1)
        return kv.reshape(rows, 64, 256).astype(out.dtype)

    for i in range(4):
        g_hb[i] = take(i, 0, 3, g_hb)
        g_ha[i] = take(i, 7, 3, g_ha)
    g_tmb[0] = take(0, 3, 4, g_tmb)
    g_own[0] = take(1, 3, 4, g_own)
    g_own[1] = take(2, 3, 4, g_own)
    g_tma[0] = take(3, 3, 4, g_tma)


def stage_body(w, x, w_out, x_out):
    w_out[...] = w[...]
    x_out[...] = x[...]


def project_body(idx, x0, x1, x2, x3, w, f0, f1):
    acc = None
    for i, x in enumerate((x0, x1, x2, x3)):
        at = pl.ds(pl.multiple_of(idx[i] * 256, 256), 256)
        part = [dot(x[...], w[n, at, :]) for n in (1, 2)]
        acc = part if acc is None else [a + b for a, b in zip(acc, part)]
    keys, values = (a.astype(BF16) for a in acc)
    halves = []
    for half in range(2):
        at = slice(half * 128, half * 128 + 128)
        halves += [keys[:, at], values[:, at]]
    kv = jnp.concatenate(halves, axis=1).reshape(2, 4, 64, 512)
    f0[...] = kv[0:1]
    f1[...] = kv[1:2]


def edges_body(tmb, f0, f1, tma, lo0, hi0, lo1, hi1):
    for half, (lo, hi) in enumerate(((lo0, hi0), (lo1, hi1))):
        lanes = pl.ds(half * 256, 256)
        for i, ref in enumerate((tmb, f0, f1, tma)):
            lo[i] = ref[0, 0:3, :, lanes]
            hi[i] = ref[0, 1:4, :, lanes]


def fold_body(g_tmb, g_tma, r_hb, r_ha, s_tmb, s_tma, acc):
    for g, at, s in ((g_tmb, 0, s_tmb), (g_tma, 3, s_tma)):
        acc[...] = g[...]
        acc[0, 0:3] += r_hb[at].astype(F32)
        acc[0, 1:4] += r_ha[at].astype(F32)
        s[...] = acc[...].astype(BF16)


def query_body(idx, x0, x1, x2, x3, w, out0, out1):
    acc = None
    for i, x in enumerate((x0, x1, x2, x3)):
        part = dot(x[...], w[0, pl.ds(pl.multiple_of(idx[i] * 256, 256), 256), :])
        acc = part if acc is None else acc + part
    query = acc.astype(BF16) * jnp.asarray(0.125, BF16)
    out0[...] = query[:, :128]
    out1[...] = query[:, 128:]


def back_body(idx, x0, x1, x2, x3, w, out0, out1):
    acc = None
    for i, x in enumerate((x0, x1, x2, x3)):
        part = dot(x[...], w[:, pl.ds(pl.multiple_of(idx[i] * 256, 256), 256)], NT)
        acc = part if acc is None else acc + part
    out0[...] = acc[:, :128].astype(BF16)
    out1[...] = acc[:, 128:].astype(BF16)


def mixed_body(idx, att0, att1, w, own, right, left, across):
    att = jnp.concatenate([att0[...], att1[...]], axis=1)
    for i, out in enumerate((own, right, left, across)):
        block = w[:, pl.ds(pl.multiple_of(idx[i] * 256, 256), 256)]
        out[...] = dot(att, block).astype(out.dtype)


def grad_body(idx, dq0, own0, hb0, ha0, tb0, ta0, dq1, own1, hb1, ha1, tb1, ta1, w,
              mine, right, left, across, kv):
    low = []
    for own, hb, ha, tb, ta in ((own0, hb0, ha0, tb0, ta0), (own1, hb1, ha1, tb1, ta1)):
        kv[...] = own[...]
        kv[:, 0:3] += hb[1:3].astype(F32)
        kv[:, 1:4] += ha[1:3].astype(F32)
        kv[0] += tb[0].astype(F32)
        kv[1] += ta[0].astype(F32)
        low.append(kv[...].reshape(512, 256).astype(BF16))
    dq = jnp.concatenate([dq0[...], dq1[...]], axis=1)
    dk = jnp.concatenate([low[0][:, :128], low[1][:, :128]], axis=1)
    dv = jnp.concatenate([low[0][:, 128:], low[1][:, 128:]], axis=1)
    for i, out in enumerate((mine, right, left, across)):
        at = pl.ds(pl.multiple_of(idx[i] * 256, 256), 256)
        total = dot(dq, w[0, at, :], NT)
        total = total + dot(dk, w[1, at, :], NT)
        total = total + dot(dv, w[2, at, :], NT)
        out[...] = total.astype(out.dtype)


def sum_body(a, b, c, d, out):
    total = a[...] + b[...].astype(F32) + c[...].astype(F32) + d[...].astype(F32)
    out[...] = total.astype(BF16).reshape(out.shape)


def local_call(body, outs, idx, arrays, scratch=(), flops=0, name=None, limit=8):
    vm = pl.BlockSpec(memory_space=pltpu.VMEM)
    specs = [vm] * len(arrays)
    args = list(arrays)
    if idx is not None:
        specs = [pl.BlockSpec(memory_space=pltpu.SMEM)] + specs
        args = [idx] + args
    return pl.pallas_call(
        body,
        out_shape=tuple(outs),
        in_specs=specs,
        out_specs=(vm,) * len(outs),
        scratch_shapes=list(scratch),
        compiler_params=pltpu.CompilerParams(vmem_limit_bytes=limit * MIB),
        cost_estimate=pl.CostEstimate(flops=flops, bytes_accessed=0, transcendentals=0),
        name=name,
    )(*args)


def shards(tokens, cotangent, w_qkv, w_out):
    S = jax.ShapeDtypeStruct
    n_x, n_t, n_h = (lax.axis_size(a) for a in ("tensor", "tm", "height"))
    x, t, h = (lax.axis_index(a) for a in ("tensor", "tm", "height"))
    idx = jnp.stack([x, (x + n_x - 1) % n_x, (x + 1) % n_x, (x + 2) % n_x]).astype(jnp.int32)
    idx_out = jnp.stack([x, (x + 1) % n_x, (x + n_x - 1) % n_x, (x + 2) % n_x]).astype(jnp.int32)
    frame_place = t * 2 + jnp.arange(4, dtype=jnp.int32) - 1
    row_place = h * 4 + jnp.arange(10, dtype=jnp.int32) - 3
    fine = ((frame_place >= 0) & (frame_place < 2 * n_t))[:, None]
    fine = fine & ((row_place >= 0) & (row_place < 4 * n_h))[None, :]
    valid = fine.astype(jnp.int32)

    def ring(array, by):
        return lax.ppermute(array, "tensor", [(i, (i + by) % n_x) for i in range(n_x)])

    def frames(array, by):
        return lax.ppermute(array, "tm", [(i, (i + by) % n_t) for i in range(n_t)])

    def rows(array, by):
        return lax.ppermute(array, "height", [(i, (i + by) % n_h) for i in range(n_h)])

    pair, frame, edge = (2, 4, 64, 256), (1, 4, 64, 256), (4, 3, 64, 256)
    half = S((512, 128), BF16)
    piece = S((512, 256), BF16)
    tok = tokens.reshape(512, 256)
    cot = cotangent.reshape(512, 256)
    t_parts = (ring(tok, 1), ring(tok, -1), ring(tok, 2))
    flat = jnp.transpose(w_qkv, (1, 0, 2))
    w_near, tok_near = local_call(stage_body, (S(flat.shape, BF16), piece), None, (flat, tok), name="stage")
    wide = S((1, 4, 64, 512), BF16)
    f0, f1 = local_call(
        project_body, (wide, wide),
        idx, (tok_near, *t_parts, w_near), name="project",
    )
    tmb, tma = frames(f1, 1), frames(f0, -1)
    tok_late, _ = lax.optimization_barrier((tok_near, f0))
    q0, q1 = local_call(
        query_body, (half, half), idx, (tok_late, *t_parts, w_near), name="query",
    )
    cot_late, _ = lax.optimization_barrier((cot, f0))
    c_parts = (ring(cot_late, 1), ring(cot_late, -1), ring(cot_late, 2))
    tmb, tma, c_parts = lax.optimization_barrier((tmb, tma, c_parts))
    b0, b1 = local_call(
        back_body, (half, half), idx, (cot, *c_parts, w_out),
        name="back",
    )
    lo0, hi0, lo1, hi1 = local_call(
        edges_body, (S(edge, BF16),) * 4, None, (tmb, f0, f1, tma), name="edges"
    )
    hb0, ha0 = rows(hi0, 1), rows(lo0, -1)
    hi1, lo1, hb0, ha0 = lax.optimization_barrier((hi1, lo1, hb0, ha0))
    hb1, ha1 = rows(hi1, 1), rows(lo1, -1)

    def attend(n, q, b, *around):
        return local_call(
            functools.partial(attend_body, n),
            (half, half, S(pair, F32), S(frame, F32), S(frame, F32), S(edge, BF16), S(edge, BF16)),
            valid, (q, b, *around),
            scratch=[
                pltpu.VMEM((2560, 128), BF16), pltpu.VMEM((2560, 128), BF16),
                pltpu.VMEM((128, 2560), BF16), pltpu.VMEM((128, 2560), BF16),
                pltpu.VMEM((2560, 128), F32), pltpu.VMEM((2560, 128), F32),
                pltpu.VMEM((1536, 256), F32), pltpu.VMEM((1536, 256), F32),
                pltpu.VMEM((1536, 256), BF16), pltpu.VMEM((1536, 256), BF16),
                pltpu.VMEM((1536, 256), BF16), pltpu.VMEM((1536, 256), BF16),
                pltpu.VMEM((4, 64, 256), F32),
            ],
            flops=4 * 6 * 2 * 1536 * 256 * 256 * 2, name="attend", limit=20,
        )

    def settle(g_tmb, g_tma, g_hb, g_ha):
        r_ha, r_hb = rows(g_hb, -1), rows(g_ha, 1)
        s_tmb, s_tma = local_call(
            fold_body, (S(frame, BF16),) * 2, None, (g_tmb, g_tma, r_hb, r_ha),
            scratch=[pltpu.VMEM(frame, F32)], name="fold",
        )
        return r_hb, r_ha, frames(s_tma, 1), frames(s_tmb, -1), s_tma

    att0, dq0, g_own0, *g0 = attend(0, q0, b0, f0, f1, tmb, tma, hb0, ha0)
    att1, dq1, g_own1, *g1 = attend(1, q1, b1, f0, f1, tmb, tma, hb1, ha1)
    back0 = settle(*g0)
    att0, _ = lax.optimization_barrier((att0, back0[4]))
    back0 = back0[:4]
    back1 = settle(*g1)[:4]
    parts = (S((512, 256), F32), piece, piece, piece)
    m0, m1, m2, m3 = local_call(
        mixed_body, parts, idx_out, (att0, att1, w_out), name="mix",
    )
    out = (S((2, 4, 64, 256), BF16),)
    (mixed,) = local_call(
        sum_body, out, None, (m0, ring(m1, 1), ring(m2, -1), ring(m3, 2)), name="mixed_sum"
    )
    e0, e1, e2, e3 = local_call(
        grad_body, parts, idx_out, (dq0, g_own0, *back0, dq1, g_own1, *back1, flat),
        scratch=[pltpu.VMEM(pair, F32)], name="in_grad", limit=14,
    )
    (in_grad,) = local_call(
        sum_body, out, None, (e0, ring(e1, 1), ring(e2, -1), ring(e3, 2)), name="in_grad_sum"
    )
    return mixed, in_grad


def solution(mesh):
    in_specs = (
        P("tm", "height", None, "tensor"),
        P("tm", "height", None, "tensor"),
        P(None, None, "tensor"),
        P("tensor", None),
    )
    out_specs = (P("tm", "height", None, "tensor"), P("tm", "height", None, "tensor"))
    return jax.shard_map(shards, mesh=mesh, in_specs=in_specs, out_specs=out_specs, check_vma=False)
```

```python
import functools
import math

import jax
import jax.numpy as jnp
from jax import lax
from jax.experimental import pallas as pl
from jax.experimental.pallas import tpu as pltpu
from jax.sharding import PartitionSpec as P

NT = (((1,), (1,)), ((), ()))
NN = (((1,), (0,)), ((), ()))
F32, BF16 = jnp.float32, jnp.bfloat16
NEG_FILL = -1e30
MIB = 1024 * 1024


def dot(a, b, dims=NN):
    return lax.dot_general(a, b, dims, preferred_element_type=F32)


def attend_body(half, valid, q, b, f0, f1, tmb, tma, hb, ha,
                att, dq, g_own, g_tmb, g_tma, g_hb, g_ha,
                ks, vs, kt, vt, dk, dv, s_buf0, s_buf1, p_buf0, p_buf1, d_buf0, d_buf1, bias):
    def put(frame, row, block):
        rows = block.shape[0]
        block = block.reshape(rows * 64, 256)
        at = pl.ds((frame * 10 + row) * 64, rows * 64)
        ks[at, :] = block[:, :128]
        vs[at, :] = block[:, 128:]

    for i in range(4):
        put(i, 0, hb[i])
        put(i, 7, ha[i])
    lanes = pl.ds(half * 256, 256)
    for i, ref in enumerate((tmb, f0, f1, tma)):
        put(i, 3, ref[0, :, :, lanes])

    vt[pl.ds(128, 16), :] = jnp.ones((16, 2560), BF16)
    eye = jnp.where(
        lax.broadcasted_iota(jnp.int32, (128, 128), 0) == lax.broadcasted_iota(jnp.int32, (128, 128), 1),
        1.0, 0.0,
    ).astype(BF16)
    same_head = (lax.broadcasted_iota(jnp.int32, (256, 128), 0) // 128) == (
        lax.broadcasted_iota(jnp.int32, (256, 128), 1) // 64
    )
    for i in range(5):
        at = pl.ds(i * 512, 512)
        kt[:, at] = ks[at, :].T
        vt[pl.ds(0, 128), at] = vs[at, :].T
    krow = lax.broadcasted_iota(jnp.int32, (64, 256), 0)
    lane = lax.broadcasted_iota(jnp.int32, (64, 256), 1)
    band = jnp.abs(krow - lane % 64) <= 3
    second = (lane // 64) % 2 == 1
    bias[0] = jnp.full((64, 256), NEG_FILL, F32)
    bias[1] = jnp.where(band, 0.0, NEG_FILL)
    bias[2] = jnp.where(band & ~second, 0.0, NEG_FILL)
    bias[3] = jnp.where(band & second, 0.0, NEG_FILL)
    first_head = lax.broadcasted_iota(jnp.int32, (128, 128), 1) < 64

    def spread(rows):
        return jnp.where(same_head, jnp.concatenate([rows] * 2, axis=0), jnp.zeros((), BF16))

    def gather(outT):
        out = outT.T
        return jnp.where(first_head, out[0:128], out[128:256])

    bufs = ((s_buf0, p_buf0, d_buf0), (s_buf1, p_buf1, d_buf1))

    def span(g, i):
        f, r = g // 2, (g % 2) * 2
        return ((f + i) * 10 + r) * 64

    def keys_of(g, i):
        return pl.ds(span(g, i), 512)

    def add_to(ref, g, i, term):
        f, r = g // 2, (g % 2) * 2
        seen = 6 if r == 2 else 0
        if f == 1 and i < 2:
            seen = 8
        at = span(g, i)
        if seen:
            ref[pl.ds(at, seen * 64), :] += term[: seen * 64]
        if seen < 8:
            ref[pl.ds(at + seen * 64, 512 - seen * 64), :] = term[seen * 64:]

    def scores(g):
        s_buf = bufs[g % 2][0]
        f, r = g // 2, (g % 2) * 2
        qbd = spread(q[pl.ds(g * 128, 128), :])
        top = jnp.full((64, 256), NEG_FILL, F32)
        for i in range(3):
            sc = dot(ks[keys_of(g, i), :], qbd, NT)
            for j in range(8):
                kind = 2 if j == 0 else 3 if j == 7 else 1
                v = sc[j * 64:(j + 1) * 64] + bias[valid[f + i, r + j] * kind]
                s_buf[pl.ds((i * 8 + j) * 64, 64), :] = v
                top = jnp.maximum(top, v)
        return jnp.max(top, axis=0, keepdims=True)

    def weights(g, m):
        s_buf, p_buf, _ = bufs[g % 2]
        tot = jnp.zeros((64, 256), F32)
        for j in range(24):
            at = pl.ds(j * 64, 64)
            e = jnp.exp(s_buf[at, :] - m)
            s_buf[at, :] = e
            tot = tot + e
        inv = 1.0 / jnp.sum(tot, axis=0, keepdims=True)
        for j in range(24):
            at = pl.ds(j * 64, 64)
            p_buf[at, :] = (s_buf[at, :] * inv).astype(BF16)
        return inv

    def values(g):
        p_buf = bufs[g % 2][1]
        mine = pl.ds(g * 128, 128)
        bbd = spread(b[mine, :])
        sums = jnp.zeros((144, 256), F32)
        for i in range(3):
            pb = p_buf[pl.ds(i * 512, 512), :]
            sums = sums + dot(vt[:, keys_of(g, i)], pb)
            add_to(dv, g, i, dot(pb, bbd))
        outT = sums[:128]
        att[mine, :] = gather(outT).astype(BF16)
        return jnp.sum(outT * dot(eye, bbd, NT), axis=0, keepdims=True) / sums[128:129]

    def slopes(g, inv, c):
        s_buf, _, d_buf = bufs[g % 2]
        bbd = spread(b[pl.ds(g * 128, 128), :])
        for i in range(3):
            sl = dot(vs[keys_of(g, i), :], bbd, NT)
            for j in range(8):
                at = pl.ds((i * 8 + j) * 64, 64)
                d_buf[at, :] = (s_buf[at, :] * inv * (sl[j * 64:(j + 1) * 64] - c)).astype(BF16)

    def grads(g):
        d_buf = bufs[g % 2][2]
        mine = pl.ds(g * 128, 128)
        qbd = spread(q[mine, :])
        dqT = jnp.zeros((128, 256), F32)
        for i in range(3):
            db = d_buf[pl.ds(i * 512, 512), :]
            dqT = dqT + dot(kt[:, keys_of(g, i)], db)
            add_to(dk, g, i, dot(db, qbd))
        dq[mine, :] = (gather(dqT) * 0.125).astype(BF16)

    m = scores(0)
    for g in range(4):
        inv = weights(g, m)
        if g > 0:
            grads(g - 1)
        if g < 3:
            m = scores(g + 1)
        c = values(g)
        slopes(g, inv, c)
    grads(3)

    def take(frame, row, rows, out):
        at = pl.ds((frame * 10 + row) * 64, rows * 64)
        kv = jnp.concatenate([dk[at, :], dv[at, :]], axis=1)
        return kv.reshape(rows, 64, 256).astype(out.dtype)

    for i in range(4):
        g_hb[i] = take(i, 0, 3, g_hb)
        g_ha[i] = take(i, 7, 3, g_ha)
    g_tmb[0] = take(0, 3, 4, g_tmb)
    g_own[0] = take(1, 3, 4, g_own)
    g_own[1] = take(2, 3, 4, g_own)
    g_tma[0] = take(3, 3, 4, g_tma)


def stage_body(w, x, w_out, x_out):
    w_out[...] = w[...]
    x_out[...] = x[...]


def project_body(idx, x0, x1, x2, x3, w, f0, f1):
    acc = None
    for i, x in enumerate((x0, x1, x2, x3)):
        at = pl.ds(pl.multiple_of(idx[i] * 256, 256), 256)
        part = [dot(x[...], w[n, at, :]) for n in (1, 2)]
        acc = part if acc is None else [a + b for a, b in zip(acc, part)]
    keys, values = (a.astype(BF16) for a in acc)
    halves = []
    for half in range(2):
        at = slice(half * 128, half * 128 + 128)
        halves += [keys[:, at], values[:, at]]
    kv = jnp.concatenate(halves, axis=1).reshape(2, 4, 64, 512)
    f0[...] = kv[0:1]
    f1[...] = kv[1:2]


def edges_body(tmb, f0, f1, tma, lo0, hi0, lo1, hi1):
    for half, (lo, hi) in enumerate(((lo0, hi0), (lo1, hi1))):
        lanes = pl.ds(half * 256, 256)
        for i, ref in enumerate((tmb, f0, f1, tma)):
            lo[i] = ref[0, 0:3, :, lanes]
            hi[i] = ref[0, 1:4, :, lanes]


def fold_body(g_tmb, g_tma, r_hb, r_ha, s_tmb, s_tma, acc):
    for g, at, s in ((g_tmb, 0, s_tmb), (g_tma, 3, s_tma)):
        acc[...] = g[...]
        acc[0, 0:3] += r_hb[at].astype(F32)
        acc[0, 1:4] += r_ha[at].astype(F32)
        s[...] = acc[...].astype(BF16)


def query_body(idx, x0, x1, x2, x3, w, out0, out1):
    acc = None
    for i, x in enumerate((x0, x1, x2, x3)):
        part = dot(x[...], w[0, pl.ds(pl.multiple_of(idx[i] * 256, 256), 256), :])
        acc = part if acc is None else acc + part
    query = acc.astype(BF16) * jnp.asarray(0.125, BF16)
    out0[...] = query[:, :128]
    out1[...] = query[:, 128:]


def back_body(idx, x0, x1, x2, x3, w, out0, out1):
    acc = None
    for i, x in enumerate((x0, x1, x2, x3)):
        part = dot(x[...], w[:, pl.ds(pl.multiple_of(idx[i] * 256, 256), 256)], NT)
        acc = part if acc is None else acc + part
    out0[...] = acc[:, :128].astype(BF16)
    out1[...] = acc[:, 128:].astype(BF16)


def mixed_body(idx, att0, att1, w, own, right, left, across):
    att = jnp.concatenate([att0[...], att1[...]], axis=1)
    for i, out in enumerate((own, right, left, across)):
        block = w[:, pl.ds(pl.multiple_of(idx[i] * 256, 256), 256)]
        out[...] = dot(att, block).astype(out.dtype)


def grad_body(idx, dq0, own0, hb0, ha0, tb0, ta0, dq1, own1, hb1, ha1, tb1, ta1, w,
              mine, right, left, across, kv):
    low = []
    for own, hb, ha, tb, ta in ((own0, hb0, ha0, tb0, ta0), (own1, hb1, ha1, tb1, ta1)):
        kv[...] = own[...]
        kv[:, 0:3] += hb[1:3].astype(F32)
        kv[:, 1:4] += ha[1:3].astype(F32)
        kv[0] += tb[0].astype(F32)
        kv[1] += ta[0].astype(F32)
        low.append(kv[...].reshape(512, 256).astype(BF16))
    dq = jnp.concatenate([dq0[...], dq1[...]], axis=1)
    dk = jnp.concatenate([low[0][:, :128], low[1][:, :128]], axis=1)
    dv = jnp.concatenate([low[0][:, 128:], low[1][:, 128:]], axis=1)
    for i, out in enumerate((mine, right, left, across)):
        at = pl.ds(pl.multiple_of(idx[i] * 256, 256), 256)
        total = dot(dq, w[0, at, :], NT)
        total = total + dot(dk, w[1, at, :], NT)
        total = total + dot(dv, w[2, at, :], NT)
        out[...] = total.astype(out.dtype)


def sum_body(a, b, c, d, out):
    total = a[...] + b[...].astype(F32) + c[...].astype(F32) + d[...].astype(F32)
    out[...] = total.astype(BF16).reshape(out.shape)


def local_call(body, outs, idx, arrays, scratch=(), flops=0, name=None, limit=8):
    vm = pl.BlockSpec(memory_space=pltpu.VMEM)
    specs = [vm] * len(arrays)
    args = list(arrays)
    if idx is not None:
        specs = [pl.BlockSpec(memory_space=pltpu.SMEM)] + specs
        args = [idx] + args
    return pl.pallas_call(
        body,
        out_shape=tuple(outs),
        in_specs=specs,
        out_specs=(vm,) * len(outs),
        scratch_shapes=list(scratch),
        compiler_params=pltpu.CompilerParams(vmem_limit_bytes=limit * MIB),
        cost_estimate=pl.CostEstimate(flops=flops, bytes_accessed=0, transcendentals=0),
        name=name,
    )(*args)


def shards(tokens, cotangent, w_qkv, w_out):
    S = jax.ShapeDtypeStruct
    n_x, n_t, n_h = (lax.axis_size(a) for a in ("tensor", "tm", "height"))
    x, t, h = (lax.axis_index(a) for a in ("tensor", "tm", "height"))
    idx = jnp.stack([x, (x + n_x - 1) % n_x, (x + 1) % n_x, (x + 2) % n_x]).astype(jnp.int32)
    idx_out = jnp.stack([x, (x + 1) % n_x, (x + n_x - 1) % n_x, (x + 2) % n_x]).astype(jnp.int32)
    frame_place = t * 2 + jnp.arange(4, dtype=jnp.int32) - 1
    row_place = h * 4 + jnp.arange(10, dtype=jnp.int32) - 3
    fine = ((frame_place >= 0) & (frame_place < 2 * n_t))[:, None]
    fine = fine & ((row_place >= 0) & (row_place < 4 * n_h))[None, :]
    valid = fine.astype(jnp.int32)

    def ring(array, by):
        return lax.ppermute(array, "tensor", [(i, (i + by) % n_x) for i in range(n_x)])

    def frames(array, by):
        return lax.ppermute(array, "tm", [(i, (i + by) % n_t) for i in range(n_t)])

    def rows(array, by):
        return lax.ppermute(array, "height", [(i, (i + by) % n_h) for i in range(n_h)])

    pair, frame, edge = (2, 4, 64, 256), (1, 4, 64, 256), (4, 3, 64, 256)
    half = S((512, 128), BF16)
    piece = S((512, 256), BF16)
    tok = tokens.reshape(512, 256)
    cot = cotangent.reshape(512, 256)
    t_parts = (ring(tok, 1), ring(tok, -1), ring(tok, 2))
    flat = jnp.transpose(w_qkv, (1, 0, 2))
    w_near, tok_near = local_call(stage_body, (S(flat.shape, BF16), piece), None, (flat, tok), name="stage")
    wide = S((1, 4, 64, 512), BF16)
    f0, f1 = local_call(
        project_body, (wide, wide),
        idx, (tok_near, *t_parts, w_near), name="project",
    )
    tmb, tma = frames(f1, 1), frames(f0, -1)
    tok_late, _ = lax.optimization_barrier((tok_near, f0))
    q0, q1 = local_call(
        query_body, (half, half), idx, (tok_late, *t_parts, w_near), name="query",
    )
    cot_late, _ = lax.optimization_barrier((cot, f0))
    c_parts = (ring(cot_late, 1), ring(cot_late, -1), ring(cot_late, 2))
    tmb, tma, c_parts = lax.optimization_barrier((tmb, tma, c_parts))
    b0, b1 = local_call(
        back_body, (half, half), idx, (cot, *c_parts, w_out),
        name="back",
    )
    lo0, hi0, lo1, hi1 = local_call(
        edges_body, (S(edge, BF16),) * 4, None, (tmb, f0, f1, tma), name="edges"
    )
    hb0, ha0 = rows(hi0, 1), rows(lo0, -1)
    hi1, lo1, hb0, ha0 = lax.optimization_barrier((hi1, lo1, hb0, ha0))
    hb1, ha1 = rows(hi1, 1), rows(lo1, -1)

    def attend(n, q, b, *around):
        return local_call(
            functools.partial(attend_body, n),
            (half, half, S(pair, F32), S(frame, F32), S(frame, F32), S(edge, BF16), S(edge, BF16)),
            valid, (q, b, *around),
            scratch=[
                pltpu.VMEM((2560, 128), BF16), pltpu.VMEM((2560, 128), BF16),
                pltpu.VMEM((128, 2560), BF16), pltpu.VMEM((144, 2560), BF16),
                pltpu.VMEM((2560, 128), F32), pltpu.VMEM((2560, 128), F32),
                pltpu.VMEM((1536, 256), F32), pltpu.VMEM((1536, 256), F32),
                pltpu.VMEM((1536, 256), BF16), pltpu.VMEM((1536, 256), BF16),
                pltpu.VMEM((1536, 256), BF16), pltpu.VMEM((1536, 256), BF16),
                pltpu.VMEM((4, 64, 256), F32),
            ],
            flops=4 * 6 * 2 * 1536 * 256 * 256 * 2, name="attend", limit=20,
        )

    def settle(g_tmb, g_tma, g_hb, g_ha):
        r_ha, r_hb = rows(g_hb, -1), rows(g_ha, 1)
        s_tmb, s_tma = local_call(
            fold_body, (S(frame, BF16),) * 2, None, (g_tmb, g_tma, r_hb, r_ha),
            scratch=[pltpu.VMEM(frame, F32)], name="fold",
        )
        return r_hb, r_ha, frames(s_tma, 1), frames(s_tmb, -1), s_tma

    att0, dq0, g_own0, *g0 = attend(0, q0, b0, f0, f1, tmb, tma, hb0, ha0)
    att1, dq1, g_own1, *g1 = attend(1, q1, b1, f0, f1, tmb, tma, hb1, ha1)
    back0 = settle(*g0)
    att0, _ = lax.optimization_barrier((att0, back0[4]))
    back0 = back0[:4]
    back1 = settle(*g1)[:4]
    parts = (S((512, 256), F32), piece, piece, piece)
    m0, m1, m2, m3 = local_call(
        mixed_body, parts, idx_out, (att0, att1, w_out), name="mix",
    )
    out = (S((2, 4, 64, 256), BF16),)
    (mixed,) = local_call(
        sum_body, out, None, (m0, ring(m1, 1), ring(m2, -1), ring(m3, 2)), name="mixed_sum"
    )
    e0, e1, e2, e3 = local_call(
        grad_body, parts, idx_out, (dq0, g_own0, *back0, dq1, g_own1, *back1, flat),
        scratch=[pltpu.VMEM(pair, F32)], name="in_grad", limit=14,
    )
    (in_grad,) = local_call(
        sum_body, out, None, (e0, ring(e1, 1), ring(e2, -1), ring(e3, 2)), name="in_grad_sum"
    )
    return mixed, in_grad


def solution(mesh):
    in_specs = (
        P("tm", "height", None, "tensor"),
        P("tm", "height", None, "tensor"),
        P(None, None, "tensor"),
        P("tensor", None),
    )
    out_specs = (P("tm", "height", None, "tensor"), P("tm", "height", None, "tensor"))
    return jax.shard_map(shards, mesh=mesh, in_specs=in_specs, out_specs=out_specs, check_vma=False)
```

```python
import functools
import math

import jax
import jax.numpy as jnp
from jax import lax
from jax.experimental import pallas as pl
from jax.experimental.pallas import tpu as pltpu
from jax.sharding import PartitionSpec as P

NT = (((1,), (1,)), ((), ()))
NN = (((1,), (0,)), ((), ()))
F32, BF16 = jnp.float32, jnp.bfloat16
NEG_FILL = -1e30
MIB = 1024 * 1024


def dot(a, b, dims=NN):
    return lax.dot_general(a, b, dims, preferred_element_type=F32)


def attend_body(half, valid, q, b, f0, f1, tmb, tma, hb, ha,
                att, dq, g_own, g_tmb, g_tma, g_hb, g_ha,
                ks, vs, kt, vt, dk, dv, s_buf0, s_buf1, p_buf0, p_buf1, d_buf0, d_buf1, bias):
    def put(frame, row, block):
        rows = block.shape[0]
        block = block.reshape(rows * 64, 256)
        at = pl.ds((frame * 10 + row) * 64, rows * 64)
        ks[at, :] = block[:, :128]
        vs[at, :] = block[:, 128:]

    for i in range(4):
        put(i, 0, hb[i])
        put(i, 7, ha[i])
    lanes = pl.ds(half * 256, 256)
    for i, ref in enumerate((tmb, f0, f1, tma)):
        put(i, 3, ref[0, :, :, lanes])

    vt[pl.ds(128, 16), :] = jnp.ones((16, 2560), BF16)
    eye = jnp.where(
        lax.broadcasted_iota(jnp.int32, (128, 128), 0) == lax.broadcasted_iota(jnp.int32, (128, 128), 1),
        1.0, 0.0,
    ).astype(BF16)
    same_head = (lax.broadcasted_iota(jnp.int32, (256, 128), 0) // 128) == (
        lax.broadcasted_iota(jnp.int32, (256, 128), 1) // 64
    )
    for i in range(5):
        at = pl.ds(i * 512, 512)
        kt[:, at] = ks[at, :].T
        vt[pl.ds(0, 128), at] = vs[at, :].T
    krow = lax.broadcasted_iota(jnp.int32, (64, 256), 0)
    lane = lax.broadcasted_iota(jnp.int32, (64, 256), 1)
    band = jnp.abs(krow - lane % 64) <= 3
    second = (lane // 64) % 2 == 1
    bias[0] = jnp.full((64, 256), NEG_FILL, F32)
    bias[1] = jnp.where(band, 0.0, NEG_FILL)
    bias[2] = jnp.where(band & ~second, 0.0, NEG_FILL)
    bias[3] = jnp.where(band & second, 0.0, NEG_FILL)
    first_head = lax.broadcasted_iota(jnp.int32, (128, 128), 1) < 64

    def spread(rows):
        return jnp.where(same_head, jnp.concatenate([rows] * 2, axis=0), jnp.zeros((), BF16))

    def gather(outT):
        out = outT.T
        return jnp.where(first_head, out[0:128], out[128:256])

    bufs = ((s_buf0, p_buf0, d_buf0), (s_buf1, p_buf1, d_buf1))

    def span(g, i):
        f, r = g // 2, (g % 2) * 2
        return ((f + i) * 10 + r) * 64

    def keys_of(g, i):
        return pl.ds(span(g, i), 512)

    def add_to(ref, g, i, term):
        f, r = g // 2, (g % 2) * 2
        seen = 6 if r == 2 else 0
        if f == 1 and i < 2:
            seen = 8
        at = span(g, i)
        if seen:
            ref[pl.ds(at, seen * 64), :] += term[: seen * 64]
        if seen < 8:
            ref[pl.ds(at + seen * 64, 512 - seen * 64), :] = term[seen * 64:]

    def scores(g):
        s_buf = bufs[g % 2][0]
        f, r = g // 2, (g % 2) * 2
        qbd = spread(q[pl.ds(g * 128, 128), :])
        top = jnp.full((64, 256), NEG_FILL, F32)
        for i in range(3):
            sc = dot(ks[keys_of(g, i), :], qbd, NT)
            for j in range(8):
                kind = 2 if j == 0 else 3 if j == 7 else 1
                v = sc[j * 64:(j + 1) * 64] + bias[valid[f + i, r + j] * kind]
                s_buf[pl.ds((i * 8 + j) * 64, 64), :] = v
                top = jnp.maximum(top, v)
        return jnp.max(top, axis=0, keepdims=True)

    def weights(g, m):
        s_buf, p_buf, _ = bufs[g % 2]
        tot = jnp.zeros((64, 256), F32)
        for j in range(24):
            at = pl.ds(j * 64, 64)
            e = jnp.exp(s_buf[at, :] - m)
            s_buf[at, :] = e
            tot = tot + e
        inv = 1.0 / jnp.sum(tot, axis=0, keepdims=True)
        for j in range(24):
            at = pl.ds(j * 64, 64)
            p_buf[at, :] = (s_buf[at, :] * inv).astype(BF16)
        return inv

    def values(g):
        p_buf = bufs[g % 2][1]
        mine = pl.ds(g * 128, 128)
        bbd = spread(b[mine, :])
        sums = jnp.zeros((144, 256), F32)
        for i in range(3):
            pb = p_buf[pl.ds(i * 512, 512), :]
            sums = sums + dot(vt[:, keys_of(g, i)], pb)
            add_to(dv, g, i, dot(pb, bbd))
        outT = sums[:128]
        att[mine, :] = gather(outT).astype(BF16)
        return jnp.sum(outT * dot(eye, bbd, NT), axis=0, keepdims=True) / sums[128:129]

    def slopes(g, inv, c):
        s_buf, _, d_buf = bufs[g % 2]
        bbd = spread(b[pl.ds(g * 128, 128), :])
        for i in range(3):
            sl = dot(vs[keys_of(g, i), :], bbd, NT)
            for j in range(8):
                at = pl.ds((i * 8 + j) * 64, 64)
                d_buf[at, :] = (s_buf[at, :] * inv * (sl[j * 64:(j + 1) * 64] - c)).astype(BF16)

    def grads(g):
        d_buf = bufs[g % 2][2]
        mine = pl.ds(g * 128, 128)
        qbd = spread(q[mine, :])
        dqT = jnp.zeros((128, 256), F32)
        for i in range(3):
            db = d_buf[pl.ds(i * 512, 512), :]
            dqT = dqT + dot(kt[:, keys_of(g, i)], db)
            add_to(dk, g, i, dot(db, qbd))
        dq[mine, :] = (gather(dqT) * 0.125).astype(BF16)

    m = scores(0)
    for g in range(4):
        inv = weights(g, m)
        if g > 0:
            grads(g - 1)
        if g < 3:
            m = scores(g + 1)
        c = values(g)
        slopes(g, inv, c)
    grads(3)

    def take(frame, row, rows, out):
        at = pl.ds((frame * 10 + row) * 64, rows * 64)
        kv = jnp.concatenate([dk[at, :], dv[at, :]], axis=1)
        return kv.reshape(rows, 64, 256).astype(out.dtype)

    for i in range(4):
        g_hb[i] = take(i, 0, 3, g_hb)
        g_ha[i] = take(i, 7, 3, g_ha)
    g_tmb[0] = take(0, 3, 4, g_tmb)
    g_own[0] = take(1, 3, 4, g_own)
    g_own[1] = take(2, 3, 4, g_own)
    g_tma[0] = take(3, 3, 4, g_tma)


def stage_body(w, w_out):
    w_out[...] = w[...]


def project_body(idx, a0, a1, a2, a3, b0, b1, b2, b3, w, f0, f1):
    for parts, out in (((a0, a1, a2, a3), f0), ((b0, b1, b2, b3), f1)):
        acc = None
        for i, x in enumerate(parts):
            at = pl.ds(pl.multiple_of(idx[i] * 256, 256), 256)
            part = [dot(x[...], w[n, at, :]) for n in (1, 2)]
            acc = part if acc is None else [a + b for a, b in zip(acc, part)]
        keys, values = (a.astype(BF16) for a in acc)
        halves = []
        for half in range(2):
            at = slice(half * 128, half * 128 + 128)
            halves += [keys[:, at], values[:, at]]
        out[...] = jnp.concatenate(halves, axis=1).reshape(1, 4, 64, 512)


def edges_body(tmb, f0, f1, tma, lo0, hi0, lo1, hi1):
    for half, (lo, hi) in enumerate(((lo0, hi0), (lo1, hi1))):
        lanes = pl.ds(half * 256, 256)
        for i, ref in enumerate((tmb, f0, f1, tma)):
            lo[i] = ref[0, 0:3, :, lanes]
            hi[i] = ref[0, 1:4, :, lanes]


def fold_body(g_tmb, g_tma, r_hb, r_ha, s_tmb, s_tma, acc):
    for g, at, s in ((g_tmb, 0, s_tmb), (g_tma, 3, s_tma)):
        acc[...] = g[...]
        acc[0, 0:3] += r_hb[at].astype(F32)
        acc[0, 1:4] += r_ha[at].astype(F32)
        s[...] = acc[...].astype(BF16)


def query_body(idx, a0, a1, a2, a3, b0, b1, b2, b3, w, out0, out1):
    for f, parts in enumerate(((a0, a1, a2, a3), (b0, b1, b2, b3))):
        acc = None
        for i, x in enumerate(parts):
            part = dot(x[...], w[0, pl.ds(pl.multiple_of(idx[i] * 256, 256), 256), :])
            acc = part if acc is None else acc + part
        query = acc.astype(BF16) * jnp.asarray(0.125, BF16)
        at = pl.ds(f * 256, 256)
        out0[at, :] = query[:, :128]
        out1[at, :] = query[:, 128:]


def back_body(idx, x0, x1, x2, x3, w, out0, out1):
    acc = None
    for i, x in enumerate((x0, x1, x2, x3)):
        part = dot(x[...], w[:, pl.ds(pl.multiple_of(idx[i] * 256, 256), 256)], NT)
        acc = part if acc is None else acc + part
    out0[...] = acc[:, :128].astype(BF16)
    out1[...] = acc[:, 128:].astype(BF16)


def mixed_body(idx, att0, att1, w, own, right, left, across):
    att = jnp.concatenate([att0[...], att1[...]], axis=1)
    for i, out in enumerate((own, right, left, across)):
        block = w[:, pl.ds(pl.multiple_of(idx[i] * 256, 256), 256)]
        out[...] = dot(att, block).astype(out.dtype)


def grad_body(idx, dq0, own0, hb0, ha0, tb0, ta0, dq1, own1, hb1, ha1, tb1, ta1, w,
              mine, right, left, across, kv):
    low = []
    for own, hb, ha, tb, ta in ((own0, hb0, ha0, tb0, ta0), (own1, hb1, ha1, tb1, ta1)):
        kv[...] = own[...]
        kv[:, 0:3] += hb[1:3].astype(F32)
        kv[:, 1:4] += ha[1:3].astype(F32)
        kv[0] += tb[0].astype(F32)
        kv[1] += ta[0].astype(F32)
        low.append(kv[...].reshape(512, 256).astype(BF16))
    dq = jnp.concatenate([dq0[...], dq1[...]], axis=1)
    dk = jnp.concatenate([low[0][:, :128], low[1][:, :128]], axis=1)
    dv = jnp.concatenate([low[0][:, 128:], low[1][:, 128:]], axis=1)
    for i, out in enumerate((mine, right, left, across)):
        at = pl.ds(pl.multiple_of(idx[i] * 256, 256), 256)
        total = dot(dq, w[0, at, :], NT)
        total = total + dot(dk, w[1, at, :], NT)
        total = total + dot(dv, w[2, at, :], NT)
        out[...] = total.astype(out.dtype)


def sum_body(a, b, c, d, out):
    total = a[...] + b[...].astype(F32) + c[...].astype(F32) + d[...].astype(F32)
    out[...] = total.astype(BF16).reshape(out.shape)


def local_call(body, outs, idx, arrays, scratch=(), flops=0, name=None, limit=8):
    vm = pl.BlockSpec(memory_space=pltpu.VMEM)
    specs = [vm] * len(arrays)
    args = list(arrays)
    if idx is not None:
        specs = [pl.BlockSpec(memory_space=pltpu.SMEM)] + specs
        args = [idx] + args
    return pl.pallas_call(
        body,
        out_shape=tuple(outs),
        in_specs=specs,
        out_specs=(vm,) * len(outs),
        scratch_shapes=list(scratch),
        compiler_params=pltpu.CompilerParams(vmem_limit_bytes=limit * MIB),
        cost_estimate=pl.CostEstimate(flops=flops, bytes_accessed=0, transcendentals=0),
        name=name,
    )(*args)


def shards(tokens, cotangent, w_qkv, w_out):
    S = jax.ShapeDtypeStruct
    n_x, n_t, n_h = (lax.axis_size(a) for a in ("tensor", "tm", "height"))
    x, t, h = (lax.axis_index(a) for a in ("tensor", "tm", "height"))
    idx = jnp.stack([x, (x + n_x - 1) % n_x, (x + 1) % n_x, (x + 2) % n_x]).astype(jnp.int32)
    idx_out = jnp.stack([x, (x + 1) % n_x, (x + n_x - 1) % n_x, (x + 2) % n_x]).astype(jnp.int32)
    frame_place = t * 2 + jnp.arange(4, dtype=jnp.int32) - 1
    row_place = h * 4 + jnp.arange(10, dtype=jnp.int32) - 3
    fine = ((frame_place >= 0) & (frame_place < 2 * n_t))[:, None]
    fine = fine & ((row_place >= 0) & (row_place < 4 * n_h))[None, :]
    valid = fine.astype(jnp.int32)

    def ring(array, by):
        return lax.ppermute(array, "tensor", [(i, (i + by) % n_x) for i in range(n_x)])

    def frames(array, by):
        return lax.ppermute(array, "tm", [(i, (i + by) % n_t) for i in range(n_t)])

    def rows(array, by):
        return lax.ppermute(array, "height", [(i, (i + by) % n_h) for i in range(n_h)])

    pair, frame, edge = (2, 4, 64, 256), (1, 4, 64, 256), (4, 3, 64, 256)
    half = S((512, 128), BF16)
    piece = S((512, 256), BF16)
    cot = cotangent.reshape(512, 256)
    own_a, own_b = tokens[0:1].reshape(256, 256), tokens[1:2].reshape(256, 256)
    right_a, left_b = ring(own_a, 1), ring(own_b, -1)
    flat = jnp.transpose(w_qkv, (1, 0, 2))
    (w_near,) = local_call(stage_body, (S(flat.shape, BF16),), None, (flat,), name="stage")
    parts_a = (own_a, right_a, ring(own_a, -1), ring(right_a, 1))
    parts_b = (own_b, ring(own_b, 1), left_b, ring(left_b, -1))
    wide = S((1, 4, 64, 512), BF16)
    f0, f1 = local_call(
        project_body, (wide, wide),
        idx, (*parts_a, *parts_b, w_near), name="project",
    )
    tmb, tma = frames(f1, 1), frames(f0, -1)
    q0, q1 = local_call(
        query_body, (half, half), idx, (*parts_a, *parts_b, w_near), name="query",
    )
    cot_late, _ = lax.optimization_barrier((cot, f0))
    c_parts = (ring(cot_late, 1), ring(cot_late, -1), ring(cot_late, 2))
    tmb, tma, c_parts = lax.optimization_barrier((tmb, tma, c_parts))
    b0, b1 = local_call(
        back_body, (half, half), idx, (cot, *c_parts, w_out),
        name="back",
    )
    lo0, hi0, lo1, hi1 = local_call(
        edges_body, (S(edge, BF16),) * 4, None, (tmb, f0, f1, tma), name="edges"
    )
    hb0, ha0 = rows(hi0, 1), rows(lo0, -1)
    hi1, lo1, hb0, ha0 = lax.optimization_barrier((hi1, lo1, hb0, ha0))
    hb1, ha1 = rows(hi1, 1), rows(lo1, -1)

    def attend(n, q, b, *around):
        return local_call(
            functools.partial(attend_body, n),
            (half, half, S(pair, F32), S(frame, F32), S(frame, F32), S(edge, BF16), S(edge, BF16)),
            valid, (q, b, *around),
            scratch=[
                pltpu.VMEM((2560, 128), BF16), pltpu.VMEM((2560, 128), BF16),
                pltpu.VMEM((128, 2560), BF16), pltpu.VMEM((144, 2560), BF16),
                pltpu.VMEM((2560, 128), F32), pltpu.VMEM((2560, 128), F32),
                pltpu.VMEM((1536, 256), F32), pltpu.VMEM((1536, 256), F32),
                pltpu.VMEM((1536, 256), BF16), pltpu.VMEM((1536, 256), BF16),
                pltpu.VMEM((1536, 256), BF16), pltpu.VMEM((1536, 256), BF16),
                pltpu.VMEM((4, 64, 256), F32),
            ],
            flops=4 * 6 * 2 * 1536 * 256 * 256 * 2, name="attend", limit=20,
        )

    def fold(g_tmb, g_tma, r_hb, r_ha):
        return local_call(
            fold_body, (S(frame, BF16),) * 2, None, (g_tmb, g_tma, r_hb, r_ha),
            scratch=[pltpu.VMEM(frame, F32)], name="fold",
        )

    att0, dq0, g_own0, *g0 = attend(0, q0, b0, f0, f1, tmb, tma, hb0, ha0)
    att1, dq1, g_own1, *g1 = attend(1, q1, b1, f0, f1, tmb, tma, hb1, ha1)
    r_hb0, r_ha0 = rows(g0[3], 1), rows(g0[2], -1)
    r_hb1, r_ha1 = rows(g1[3], 1), rows(g1[2], -1)
    s_tmb, s_tma = fold(g0[0], g0[1], r_hb0, r_ha0)
    back0 = (r_hb0, r_ha0, frames(s_tma, 1), frames(s_tmb, -1))
    att0, _ = lax.optimization_barrier((att0, s_tma))
    parts = (S((512, 256), F32), piece, piece, piece)
    m0, m1, m2, m3 = local_call(mixed_body, parts, idx_out, (att0, att1, w_out), name="mix")
    r_hb1, r_ha1, m1, m2 = lax.optimization_barrier((r_hb1, r_ha1, ring(m1, 1), ring(m2, -1)))
    m3 = ring(m3, 2)
    s_tmb, s_tma = fold(g1[0], g1[1], r_hb1, r_ha1)
    back1 = (r_hb1, r_ha1, frames(s_tma, 1), frames(s_tmb, -1))
    out = (S((2, 4, 64, 256), BF16),)
    (mixed,) = local_call(sum_body, out, None, (m0, m1, m2, m3), name="mixed_sum")
    e0, e1, e2, e3 = local_call(
        grad_body, parts, idx_out, (dq0, g_own0, *back0, dq1, g_own1, *back1, flat),
        scratch=[pltpu.VMEM(pair, F32)], name="in_grad", limit=14,
    )
    (in_grad,) = local_call(
        sum_body, out, None, (e0, ring(e1, 1), ring(e2, -1), ring(e3, 2)), name="in_grad_sum"
    )
    return mixed, in_grad


def solution(mesh):
    in_specs = (
        P("tm", "height", None, "tensor"),
        P("tm", "height", None, "tensor"),
        P(None, None, "tensor"),
        P("tensor", None),
    )
    out_specs = (P("tm", "height", None, "tensor"), P("tm", "height", None, "tensor"))
    return jax.shard_map(shards, mesh=mesh, in_specs=in_specs, out_specs=out_specs, check_vma=False)
```

```python
import functools
import math

import jax
import jax.numpy as jnp
from jax import lax
from jax.experimental import pallas as pl
from jax.experimental.pallas import tpu as pltpu
from jax.sharding import PartitionSpec as P

NT = (((1,), (1,)), ((), ()))
NN = (((1,), (0,)), ((), ()))
F32, BF16 = jnp.float32, jnp.bfloat16
NEG_FILL = -1e30
MIB = 1024 * 1024


def dot(a, b, dims=NN):
    return lax.dot_general(a, b, dims, preferred_element_type=F32)


def attend_body(half, valid, q, b, f0, f1, tmb, tma, hb, ha,
                att, dq, g_own, g_tmb, g_tma, g_hb, g_ha,
                ks, vs, kt, vt, dk, dv, s_buf0, s_buf1, p_buf0, p_buf1, d_buf0, d_buf1, bias):
    def put(frame, row, block):
        rows = block.shape[0]
        block = block.reshape(rows * 64, 256)
        at = pl.ds((frame * 10 + row) * 64, rows * 64)
        ks[at, :] = block[:, :128]
        vs[at, :] = block[:, 128:]

    for i in range(4):
        put(i, 0, hb[i])
        put(i, 7, ha[i])
    lanes = pl.ds(half * 256, 256)
    for i, ref in enumerate((tmb, f0, f1, tma)):
        put(i, 3, ref[0, :, :, lanes])

    vt[pl.ds(128, 16), :] = jnp.ones((16, 2560), BF16)
    eye = jnp.where(
        lax.broadcasted_iota(jnp.int32, (128, 128), 0) == lax.broadcasted_iota(jnp.int32, (128, 128), 1),
        1.0, 0.0,
    ).astype(BF16)
    same_head = (lax.broadcasted_iota(jnp.int32, (256, 128), 0) // 128) == (
        lax.broadcasted_iota(jnp.int32, (256, 128), 1) // 64
    )
    for i in range(5):
        at = pl.ds(i * 512, 512)
        kt[:, at] = ks[at, :].T
        vt[pl.ds(0, 128), at] = vs[at, :].T
    krow = lax.broadcasted_iota(jnp.int32, (64, 256), 0)
    lane = lax.broadcasted_iota(jnp.int32, (64, 256), 1)
    band = jnp.abs(krow - lane % 64) <= 3
    second = (lane // 64) % 2 == 1
    bias[0] = jnp.full((64, 256), NEG_FILL, F32)
    bias[1] = jnp.where(band, 0.0, NEG_FILL)
    bias[2] = jnp.where(band & ~second, 0.0, NEG_FILL)
    bias[3] = jnp.where(band & second, 0.0, NEG_FILL)
    first_head = lax.broadcasted_iota(jnp.int32, (128, 128), 1) < 64

    def spread(rows):
        return jnp.where(same_head, jnp.concatenate([rows] * 2, axis=0), jnp.zeros((), BF16))

    def gather(outT):
        out = outT.T
        return jnp.where(first_head, out[0:128], out[128:256])

    bufs = ((s_buf0, p_buf0, d_buf0), (s_buf1, p_buf1, d_buf1))

    def span(g, i):
        f, r = g // 2, (g % 2) * 2
        return ((f + i) * 10 + r) * 64

    def keys_of(g, i):
        return pl.ds(span(g, i), 512)

    def add_to(ref, g, i, term):
        f, r = g // 2, (g % 2) * 2
        seen = 6 if r == 2 else 0
        if f == 1 and i < 2:
            seen = 8
        at = span(g, i)
        if seen:
            ref[pl.ds(at, seen * 64), :] += term[: seen * 64]
        if seen < 8:
            ref[pl.ds(at + seen * 64, 512 - seen * 64), :] = term[seen * 64:]

    def scores(g):
        s_buf = bufs[g % 2][0]
        f, r = g // 2, (g % 2) * 2
        qbd = spread(q[pl.ds(g * 128, 128), :])
        top = jnp.full((64, 256), NEG_FILL, F32)
        for i in range(3):
            sc = dot(ks[keys_of(g, i), :], qbd, NT)
            for j in range(8):
                kind = 2 if j == 0 else 3 if j == 7 else 1
                v = sc[j * 64:(j + 1) * 64] + bias[valid[f + i, r + j] * kind]
                s_buf[pl.ds((i * 8 + j) * 64, 64), :] = v
                top = jnp.maximum(top, v)
        return jnp.max(top, axis=0, keepdims=True)

    def weights(g, m):
        s_buf, p_buf, _ = bufs[g % 2]
        tot = jnp.zeros((64, 256), F32)
        for j in range(24):
            at = pl.ds(j * 64, 64)
            e = jnp.exp(s_buf[at, :] - m)
            s_buf[at, :] = e
            tot = tot + e
        inv = 1.0 / jnp.sum(tot, axis=0, keepdims=True)
        for j in range(24):
            at = pl.ds(j * 64, 64)
            p_buf[at, :] = (s_buf[at, :] * inv).astype(BF16)
        return inv

    def values(g):
        p_buf = bufs[g % 2][1]
        mine = pl.ds(g * 128, 128)
        bbd = spread(b[mine, :])
        sums = jnp.zeros((144, 256), F32)
        for i in range(3):
            pb = p_buf[pl.ds(i * 512, 512), :]
            sums = sums + dot(vt[:, keys_of(g, i)], pb)
            add_to(dv, g, i, dot(pb, bbd))
        outT = sums[:128]
        att[mine, :] = gather(outT).astype(BF16)
        return jnp.sum(outT * dot(eye, bbd, NT), axis=0, keepdims=True) / sums[128:129]

    def slopes(g, inv, c):
        s_buf, _, d_buf = bufs[g % 2]
        bbd = spread(b[pl.ds(g * 128, 128), :])
        for i in range(3):
            sl = dot(vs[keys_of(g, i), :], bbd, NT)
            for j in range(8):
                at = pl.ds((i * 8 + j) * 64, 64)
                d_buf[at, :] = (s_buf[at, :] * inv * (sl[j * 64:(j + 1) * 64] - c)).astype(BF16)

    def grads(g):
        d_buf = bufs[g % 2][2]
        mine = pl.ds(g * 128, 128)
        qbd = spread(q[mine, :])
        dqT = jnp.zeros((128, 256), F32)
        for i in range(3):
            db = d_buf[pl.ds(i * 512, 512), :]
            dqT = dqT + dot(kt[:, keys_of(g, i)], db)
            add_to(dk, g, i, dot(db, qbd))
        dq[mine, :] = (gather(dqT) * 0.125).astype(BF16)

    m = scores(0)
    for g in range(4):
        inv = weights(g, m)
        if g > 0:
            grads(g - 1)
        if g < 3:
            m = scores(g + 1)
        c = values(g)
        slopes(g, inv, c)
    grads(3)

    def take(frame, row, rows, out):
        at = pl.ds((frame * 10 + row) * 64, rows * 64)
        kv = jnp.concatenate([dk[at, :], dv[at, :]], axis=1)
        return kv.reshape(rows, 64, 256).astype(out.dtype)

    for i in range(4):
        g_hb[i] = take(i, 0, 3, g_hb)
        g_ha[i] = take(i, 7, 3, g_ha)
    g_tmb[0] = take(0, 3, 4, g_tmb)
    g_own[0] = take(1, 3, 4, g_own)
    g_own[1] = take(2, 3, 4, g_own)
    g_tma[0] = take(3, 3, 4, g_tma)


def stage_body(w, w_out):
    w_out[...] = w[...]


def project_body(idx, a0, a1, a2, a3, b0, b1, b2, b3, w, f0, f1):
    for parts, out in (((a0, a1, a2, a3), f0), ((b0, b1, b2, b3), f1)):
        acc = None
        for i, x in enumerate(parts):
            at = pl.ds(pl.multiple_of(idx[i] * 256, 256), 256)
            part = [dot(x[...], w[n, at, :]) for n in (1, 2)]
            acc = part if acc is None else [a + b for a, b in zip(acc, part)]
        keys, values = (a.astype(BF16) for a in acc)
        halves = []
        for half in range(2):
            at = slice(half * 128, half * 128 + 128)
            halves += [keys[:, at], values[:, at]]
        out[...] = jnp.concatenate(halves, axis=1).reshape(1, 4, 64, 512)


def edges_body(half, tmb, f0, f1, tma, lo, hi):
    lanes = pl.ds(half * 256, 256)
    for i, ref in enumerate((tmb, f0, f1, tma)):
        lo[i] = ref[0, 0:3, :, lanes]
        hi[i] = ref[0, 1:4, :, lanes]


def fold_body(g_tmb, g_tma, r_hb, r_ha, s_tmb, s_tma, acc):
    for g, at, s in ((g_tmb, 0, s_tmb), (g_tma, 3, s_tma)):
        acc[...] = g[...]
        acc[0, 0:3] += r_hb[at].astype(F32)
        acc[0, 1:4] += r_ha[at].astype(F32)
        s[...] = acc[...].astype(BF16)


def query_body(idx, a0, a1, a2, a3, b0, b1, b2, b3, w, out0, out1):
    for f, parts in enumerate(((a0, a1, a2, a3), (b0, b1, b2, b3))):
        acc = None
        for i, x in enumerate(parts):
            part = dot(x[...], w[0, pl.ds(pl.multiple_of(idx[i] * 256, 256), 256), :])
            acc = part if acc is None else acc + part
        query = acc.astype(BF16) * jnp.asarray(0.125, BF16)
        at = pl.ds(f * 256, 256)
        out0[at, :] = query[:, :128]
        out1[at, :] = query[:, 128:]


def back_body(idx, x0, x1, x2, x3, w, out0, out1):
    acc = None
    for i, x in enumerate((x0, x1, x2, x3)):
        part = dot(x[...], w[:, pl.ds(pl.multiple_of(idx[i] * 256, 256), 256)], NT)
        acc = part if acc is None else acc + part
    out0[...] = acc[:, :128].astype(BF16)
    out1[...] = acc[:, 128:].astype(BF16)


def mixed_body(idx, att0, att1, w, own, right, left, across):
    att = jnp.concatenate([att0[...], att1[...]], axis=1)
    for i, out in enumerate((own, right, left, across)):
        block = w[:, pl.ds(pl.multiple_of(idx[i] * 256, 256), 256)]
        out[...] = dot(att, block).astype(out.dtype)


def grad_body(idx, dq0, own0, hb0, ha0, tb0, ta0, dq1, own1, hb1, ha1, tb1, ta1, w,
              mine, right, left, across, kv):
    low = []
    for own, hb, ha, tb, ta in ((own0, hb0, ha0, tb0, ta0), (own1, hb1, ha1, tb1, ta1)):
        kv[...] = own[...]
        kv[:, 0:3] += hb[1:3].astype(F32)
        kv[:, 1:4] += ha[1:3].astype(F32)
        kv[0] += tb[0].astype(F32)
        kv[1] += ta[0].astype(F32)
        low.append(kv[...].reshape(512, 256).astype(BF16))
    dq = jnp.concatenate([dq0[...], dq1[...]], axis=1)
    dk = jnp.concatenate([low[0][:, :128], low[1][:, :128]], axis=1)
    dv = jnp.concatenate([low[0][:, 128:], low[1][:, 128:]], axis=1)
    for i, out in enumerate((mine, right, left, across)):
        at = pl.ds(pl.multiple_of(idx[i] * 256, 256), 256)
        total = dot(dq, w[0, at, :], NT)
        total = total + dot(dk, w[1, at, :], NT)
        total = total + dot(dv, w[2, at, :], NT)
        out[...] = total.astype(out.dtype)


def sum_body(a, b, c, d, out):
    total = a[...] + b[...].astype(F32) + c[...].astype(F32) + d[...].astype(F32)
    out[...] = total.astype(BF16).reshape(out.shape)


def local_call(body, outs, idx, arrays, scratch=(), flops=0, name=None, limit=8):
    vm = pl.BlockSpec(memory_space=pltpu.VMEM)
    specs = [vm] * len(arrays)
    args = list(arrays)
    if idx is not None:
        specs = [pl.BlockSpec(memory_space=pltpu.SMEM)] + specs
        args = [idx] + args
    return pl.pallas_call(
        body,
        out_shape=tuple(outs),
        in_specs=specs,
        out_specs=(vm,) * len(outs),
        scratch_shapes=list(scratch),
        compiler_params=pltpu.CompilerParams(vmem_limit_bytes=limit * MIB),
        cost_estimate=pl.CostEstimate(flops=flops, bytes_accessed=0, transcendentals=0),
        name=name,
    )(*args)


def shards(tokens, cotangent, w_qkv, w_out):
    S = jax.ShapeDtypeStruct
    n_x, n_t, n_h = (lax.axis_size(a) for a in ("tensor", "tm", "height"))
    x, t, h = (lax.axis_index(a) for a in ("tensor", "tm", "height"))
    idx = jnp.stack([x, (x + n_x - 1) % n_x, (x + 1) % n_x, (x + 2) % n_x]).astype(jnp.int32)
    idx_out = jnp.stack([x, (x + 1) % n_x, (x + n_x - 1) % n_x, (x + 2) % n_x]).astype(jnp.int32)
    frame_place = t * 2 + jnp.arange(4, dtype=jnp.int32) - 1
    row_place = h * 4 + jnp.arange(10, dtype=jnp.int32) - 3
    fine = ((frame_place >= 0) & (frame_place < 2 * n_t))[:, None]
    fine = fine & ((row_place >= 0) & (row_place < 4 * n_h))[None, :]
    valid = fine.astype(jnp.int32)

    def ring(array, by):
        return lax.ppermute(array, "tensor", [(i, (i + by) % n_x) for i in range(n_x)])

    def frames(array, by):
        return lax.ppermute(array, "tm", [(i, (i + by) % n_t) for i in range(n_t)])

    def rows(array, by):
        return lax.ppermute(array, "height", [(i, (i + by) % n_h) for i in range(n_h)])

    pair, frame, edge = (2, 4, 64, 256), (1, 4, 64, 256), (4, 3, 64, 256)
    half = S((512, 128), BF16)
    piece = S((512, 256), BF16)
    cot = cotangent.reshape(512, 256)
    own_a, own_b = tokens[0:1].reshape(256, 256), tokens[1:2].reshape(256, 256)
    right_a, left_b = ring(own_a, 1), ring(own_b, -1)
    flat = jnp.transpose(w_qkv, (1, 0, 2))
    (w_near,) = local_call(stage_body, (S(flat.shape, BF16),), None, (flat,), name="stage")
    parts_a = (own_a, right_a, ring(own_a, -1), ring(right_a, 1))
    parts_b = (own_b, ring(own_b, 1), left_b, ring(left_b, -1))
    wide = S((1, 4, 64, 512), BF16)
    f0, f1 = local_call(
        project_body, (wide, wide),
        idx, (*parts_a, *parts_b, w_near), name="project",
    )
    tmb, tma = frames(f1, 1), frames(f0, -1)
    q0, q1 = local_call(
        query_body, (half, half), idx, (*parts_a, *parts_b, w_near), name="query",
    )
    cot_late, _ = lax.optimization_barrier((cot, f0))
    c_parts = (ring(cot_late, 1), ring(cot_late, -1), ring(cot_late, 2))
    tmb, tma, c_parts = lax.optimization_barrier((tmb, tma, c_parts))
    b0, b1 = local_call(
        back_body, (half, half), idx, (cot, *c_parts, w_out),
        name="back",
    )
    def edges(n, *around):
        return local_call(
            functools.partial(edges_body, n), (S(edge, BF16),) * 2, None, around, name="edges"
        )

    lo0, hi0 = edges(0, tmb, f0, f1, tma)
    f0_late, _ = lax.optimization_barrier((f0, lo0))
    lo1, hi1 = edges(1, tmb, f0_late, f1, tma)
    hb0, ha0 = rows(hi0, 1), rows(lo0, -1)
    hi1, lo1, hb0, ha0 = lax.optimization_barrier((hi1, lo1, hb0, ha0))
    hb1, ha1 = rows(hi1, 1), rows(lo1, -1)

    def attend(n, q, b, *around):
        return local_call(
            functools.partial(attend_body, n),
            (half, half, S(pair, F32), S(frame, F32), S(frame, F32), S(edge, BF16), S(edge, BF16)),
            valid, (q, b, *around),
            scratch=[
                pltpu.VMEM((2560, 128), BF16), pltpu.VMEM((2560, 128), BF16),
                pltpu.VMEM((128, 2560), BF16), pltpu.VMEM((144, 2560), BF16),
                pltpu.VMEM((2560, 128), F32), pltpu.VMEM((2560, 128), F32),
                pltpu.VMEM((1536, 256), F32), pltpu.VMEM((1536, 256), F32),
                pltpu.VMEM((1536, 256), BF16), pltpu.VMEM((1536, 256), BF16),
                pltpu.VMEM((1536, 256), BF16), pltpu.VMEM((1536, 256), BF16),
                pltpu.VMEM((4, 64, 256), F32),
            ],
            flops=4 * 6 * 2 * 1536 * 256 * 256 * 2, name="attend", limit=20,
        )

    def fold(g_tmb, g_tma, r_hb, r_ha):
        return local_call(
            fold_body, (S(frame, BF16),) * 2, None, (g_tmb, g_tma, r_hb, r_ha),
            scratch=[pltpu.VMEM(frame, F32)], name="fold",
        )

    att0, dq0, g_own0, *g0 = attend(0, q0, b0, f0, f1, tmb, tma, hb0, ha0)
    att1, dq1, g_own1, *g1 = attend(1, q1, b1, f0, f1, tmb, tma, hb1, ha1)
    r_hb0, r_ha0 = rows(g0[3], 1), rows(g0[2], -1)
    r_hb1, r_ha1 = rows(g1[3], 1), rows(g1[2], -1)
    s_tmb, s_tma = fold(g0[0], g0[1], r_hb0, r_ha0)
    back0 = (r_hb0, r_ha0, frames(s_tma, 1), frames(s_tmb, -1))
    att0, _ = lax.optimization_barrier((att0, s_tma))
    parts = (S((512, 256), F32), piece, piece, piece)
    m0, m1, m2, m3 = local_call(mixed_body, parts, idx_out, (att0, att1, w_out), name="mix")
    r_hb1, r_ha1, m1, m2 = lax.optimization_barrier((r_hb1, r_ha1, ring(m1, 1), ring(m2, -1)))
    m3 = ring(m3, 2)
    s_tmb, s_tma = fold(g1[0], g1[1], r_hb1, r_ha1)
    back1 = (r_hb1, r_ha1, frames(s_tma, 1), frames(s_tmb, -1))
    out = (S((2, 4, 64, 256), BF16),)
    (mixed,) = local_call(sum_body, out, None, (m0, m1, m2, m3), name="mixed_sum")
    e0, e1, e2, e3 = local_call(
        grad_body, parts, idx_out, (dq0, g_own0, *back0, dq1, g_own1, *back1, flat),
        scratch=[pltpu.VMEM(pair, F32)], name="in_grad", limit=14,
    )
    (in_grad,) = local_call(
        sum_body, out, None, (e0, ring(e1, 1), ring(e2, -1), ring(e3, 2)), name="in_grad_sum"
    )
    return mixed, in_grad


def solution(mesh):
    in_specs = (
        P("tm", "height", None, "tensor"),
        P("tm", "height", None, "tensor"),
        P(None, None, "tensor"),
        P("tensor", None),
    )
    out_specs = (P("tm", "height", None, "tensor"), P("tm", "height", None, "tensor"))
    return jax.shard_map(shards, mesh=mesh, in_specs=in_specs, out_specs=out_specs, check_vma=False)
```
